256 devices in a mesh: leaf: 64 (over y, z, core), panel: 4 (over x).
Axes of the slice: x: 4, y: 4, z: 8, core: 2. Of those that a mesh axis runs over, the one named last changes fastest.
Arguments:
- sigma_tiles: bfloat16 [1024, 256, 256], P('leaf', 'panel'), may hold values from -6 to 6
- panel_factor: bfloat16 [256, 15, 256, 256], P('leaf', None, 'panel'), may hold values from -0.09375 to 0.09375
- panel_mask: int32 [256, 15], P('leaf'), may hold values 0 or 1
- inv_diagonal: float32 [256, 256], P('leaf', 'panel'), may hold values from 0.5 to 2
- subtree_of: int32 [64], replicated, may hold values from 0 to 15
- partition_order: int32 [65536], P(('leaf', 'panel')), may hold values from 0 to 65535, each once
Outputs:
- covariance: bfloat16 [256, 15, 256, 256], P('leaf', None, 'panel')
- variance: float32 [65536], P(('leaf', 'panel'))
The draws below stay inside these ranges and needn't reach their ends.
All inputs are finite; a program needn't handle non-finite values. No bound on the sum of `panel_mask` on one device may be relied on, other than what follows from the above.
Results may differ from the reference program's by a relative error of at most 0.00065.
Values may be sent and summed in bfloat16 or wider, within the bound.
A program may use at most 128 MiB of HBM per device.

```python
import math
import jax
import jax.numpy as jnp
from jax import lax

B = 256
NA = 32
CH = 15
DESC_DEV = 4
DESC_ALL = 256
NV = 65536
N_LEAF = 64


def place_ends(values, stream_key, smallest, top_value):
    shape = values.shape
    spot = [jax.random.randint(jax.random.fold_in(stream_key, axis), (), 0, shape[axis]) for axis in range(len(shape))]
    values = values.at[tuple(spot)].set(smallest)
    longest = shape.index(max(shape))
    spot[longest] = (spot[longest] + 1) % shape[longest]
    return values.at[tuple(spot)].set(top_value)


def block_scale(key, extent, shards, low, top_value):
    loudness, own = 1.0, jax.random.fold_in(key, 6)
    for position, shards_of in shards:
        heights = jnp.exp(jax.random.uniform(jax.random.fold_in(own, position), (shards_of,), jnp.float32, low / len(shards), top_value / len(shards)))
        loudness = loudness * jnp.repeat(heights, extent[position] // shards_of).reshape([-1 if axis == position else 1 for axis in range(len(extent))])
    return loudness


def bell_draw(rng, dims, scale, most, split=(), kind=jnp.bfloat16):
    drawn = jax.random.normal(rng, dims, jnp.float32) * scale
    if len(split) > 0:
        drawn = block_scale(rng, dims, split, -0.22, 0.18) * drawn
    return jnp.clip(drawn, min=-most, max=most).astype(kind)


def setup_inputs(seed: int = 0) -> dict:
    splits = jax.random.split(jax.random.key(seed), 7)
    return {
        "sigma_tiles": bell_draw(splits[0], (NA * NA, B, B), 1.0, 6.0, ((0, 64), (1, 4))),
        "panel_factor": bell_draw(splits[1], (DESC_ALL, CH, B, B), (CH * B) ** -0.5, 0.09375, ((0, 64), (2, 4))),
        "panel_mask": place_ends((jax.random.randint(splits[2], (DESC_ALL, CH), 0, 3) < 2).astype(jnp.int32), jax.random.fold_in(splits[2], 1), 0, 1),
        "inv_diagonal": jnp.clip(jnp.exp(math.log(2.0) - 1.3862944 * jax.random.uniform(splits[3], (DESC_ALL, B), jnp.float32) ** block_scale(splits[3], (DESC_ALL, B), ((0, 64), (1, 4)), -0.2, 0.2)), 0.5, 2.0),
        "subtree_of": place_ends(jax.random.randint(splits[4], (N_LEAF,), 0, 16), jax.random.fold_in(splits[4], 1), 0, 15).astype(jnp.int32),
        "partition_order": jax.random.permutation(splits[5], NV).astype(jnp.int32),
    }


def chain_blocks(subtree):
    subtree_col = subtree[..., None]
    root_ids = jnp.broadcast_to(jnp.arange(8, dtype=jnp.int32), subtree_col.shape[:-1] + (8,))
    upper_ids = 8 + 4 * (subtree_col // 8) + jnp.arange(4, dtype=jnp.int32)
    middle = 16 + 2 * (subtree_col // 4) + jnp.arange(2, dtype=jnp.int32)
    lower_ids = 24 + subtree_col // 2
    return jnp.concatenate([root_ids, upper_ids, middle, lower_ids], axis=-1).astype(jnp.int32)


def reference(sigma_tiles, panel_factor, panel_mask, inv_diagonal, subtree_of, partition_order):
    owners = jnp.repeat(subtree_of, DESC_DEV)
    masked = panel_factor * panel_mask[:, :, None, None].astype(jnp.bfloat16)

    def per_block(inputs_pair):
        subtree, factor = inputs_pair
        chain = chain_blocks(subtree)
        tile_ids = (chain[:, None] * NA + chain[None, :]).reshape(-1).astype(jnp.int32)
        sigma_block = jnp.take(sigma_tiles, tile_ids, axis=0).reshape(CH, CH, B, B).astype(jnp.float32)
        factor_wide = factor.astype(jnp.float32)
        product = jnp.einsum("abrk,bkc->arc", sigma_block, factor_wide)
        partial_value = jnp.sum(factor_wide * product, axis=(0, 1))
        return (-product).astype(jnp.bfloat16), partial_value

    covariance, partial_value = lax.map(per_block, (owners, masked))
    diag_var = (inv_diagonal + partial_value).reshape(-1)
    return covariance, jnp.take(diag_var, partition_order, axis=0)
```

```python
import jax
import jax.numpy as jnp
from jax import lax
from jax.experimental import pallas as pl
from jax.experimental.pallas import tpu as pltpu
from jax.sharding import PartitionSpec as P

NX, NY, NZ = 4, 4, 8
CH = 15
B = 256
Q = 64
DESC = 4
NEAR = 12
FAR = (20, 8, 4, 3)
FAR_AT = (0, 20, 28, 32)
COLUMN = 35
FAR_BASE = NX * NY * NZ // NX * NEAR
TILES = FAR_BASE + NZ * COLUMN
Z_ORDER = (0, -1, 1, -2, 2, -3, 3, 4)
GROUP = 5
MESH = pl.DeviceIdType.MESH


def halves(count):
    return (0, (count + 1) // 2), ((count + 1) // 2, count // 2)


def kernel(
    idx_ref, mask_ref, inv_ref, sigma_ref, factor_ref,
    cov_ref, table_ref,
    tiles, lhs, full, own, parts, table,
    send_sem, recv_sem, local_sem,
):
    leaf = lax.axis_index("leaf")
    x = lax.axis_index("panel")
    core = lax.rem(leaf, 2)
    chip = leaf // 2
    y = chip // NZ
    z = lax.rem(chip, NZ)

    def mod(value, size):
        return lax.rem(value + 2 * size, size)

    def at(dy=0, dz=0, dc=0):
        return {"leaf": (mod(y + dy, NY) * NZ + mod(z + dz, NZ)) * 2 + lax.rem(core + dc, 2), "panel": x}

    def beside(dx):
        return {"leaf": leaf, "panel": mod(x + dx, NX)}

    sends = {}
    recvs = {}
    pending = []

    def number(names, name):
        if name not in names:
            names[name] = len(names)
        return names[name]

    def copy(src, dst, device, name):
        return pltpu.make_async_remote_copy(
            src_ref=src, dst_ref=dst,
            send_sem=send_sem.at[number(sends, name)],
            recv_sem=recv_sem.at[number(recvs, name)],
            device_id=device, device_id_type=MESH,
        )

    def send(ref, device, name, src=None):
        def build():
            return copy((src or ref)(), ref(), device(), name)

        build().start()
        pending.append(build)

    def arrive(ref, name):
        copy(ref, ref, beside(1), name).wait_recv()

    for j in range(DESC):
        pltpu.make_async_copy(factor_ref.at[j], own.at[j], local_sem.at[j]).start()

    peers = (
        [beside(d) for d in range(1, NX)]
        + [at(dz=d) for d in range(1, NZ)]
        + [at(dy=d, dc=c) for d in range(NY) for c in range(2) if (d, c) != (0, 0)]
    )
    barrier = pltpu.get_barrier_semaphore()
    for peer in peers:
        pl.semaphore_signal(barrier, inc=1, device_id=peer, device_id_type=MESH)
    pl.semaphore_wait(barrier, len(peers))

    def quarter(j, dx, low=0, count=CH):
        return full.at[j, pl.ds(low, count), pl.ds(pl.multiple_of(mod(x + dx, NX) * Q, Q), Q)]

    def factor_parts(j):
        first = 8 - j % 2
        return (0, first), (first, CH - first)

    def factor_start(j):
        pltpu.make_async_copy(factor_ref.at[j], own.at[j], local_sem.at[j]).wait()
        for b in range(CH):
            own[j, b] = own[j, b] * mask_ref[j, b].astype(jnp.bfloat16)
        send(lambda: quarter(j, 0), lambda: beside(1), ("fr", j), src=lambda: own.at[j])
        send(lambda: quarter(j, 0), lambda: beside(-1), ("fl", j), src=lambda: own.at[j])
        pltpu.make_async_copy(own.at[j], quarter(j, 0), local_sem.at[DESC + j]).start()

    def factor_forward(j):
        right, left = factor_parts(j)
        arrive(quarter(j, -1), ("fr", j))
        send(lambda: quarter(j, -1, *right), lambda: beside(1), ("fr2", j))
        arrive(quarter(j, 1), ("fl", j))
        send(lambda: quarter(j, 1, *left), lambda: beside(-1), ("fl2", j))

    def factor_done(j):
        right, left = factor_parts(j)
        arrive(quarter(j, 2, *right), ("fr2", j))
        arrive(quarter(j, 2, *left), ("fl2", j))
        pltpu.make_async_copy(own.at[j], quarter(j, 0), local_sem.at[DESC + j]).wait()

    def near(dy, dz, low=0, count=NEAR):
        row = mod(y + dy, NY) * NZ + mod(z + dz, NZ)
        return tiles.at[pl.ds(row * NEAR + low, count)]

    def far(dz, low=0, count=COLUMN):
        return tiles.at[pl.ds(FAR_BASE + mod(z + dz, NZ) * COLUMN + low, count)]

    first6, last6 = halves(NEAR)
    near_chunks = [(dy, dz) for dy in range(NY) for dz in Z_ORDER]

    def run_core0():
        def to_peer(dy, dz):
            send(lambda: near(dy, dz), lambda: at(dc=1), ("n", dy % NY, dz))

        def along_y(dz):
            send(lambda: near(0, dz), lambda: at(dy=1), ("yu", dz))
            send(lambda: near(0, dz), lambda: at(dy=-1), ("yd", dz))
            to_peer(0, dz)

        def start():
            @pl.when(y == 0)
            def _():
                ref = far(0, 0, 4)
                copy(sigma_ref.at[pl.ds(12, 4)], ref, at(dc=1), ("extra",)).start()

            upper = jnp.where(y == 0, 0, z // 4)
            one = pltpu.make_async_copy(sigma_ref.at[pl.ds(0, 8)], near(0, 0, 0, 8), local_sem.at[2 * DESC])
            two = pltpu.make_async_copy(
                sigma_ref.at[pl.ds(8 + 4 * upper, 4)], near(0, 0, 8, 4), local_sem.at[2 * DESC + 1]
            )
            one.start()
            two.start()
            one.wait()
            two.wait()
            send(lambda: near(0, 0), lambda: at(dz=1), ("zr", 1))
            send(lambda: near(0, 0), lambda: at(dz=-1), ("zl", 1))
            along_y(0)

        def ring(d):
            arrive(near(0, -d), ("zr", d))
            if d < 3:
                send(lambda: near(0, -d), lambda: at(dz=1), ("zr", d + 1))
            else:
                send(lambda: near(0, -d, *first6), lambda: at(dz=1), ("zr", 4))
            arrive(near(0, d), ("zl", d))
            if d < 3:
                send(lambda: near(0, d), lambda: at(dz=-1), ("zl", d + 1))
            else:
                send(lambda: near(0, d, *last6), lambda: at(dz=-1), ("zl", 4))
            along_y(-d)
            along_y(d)

        def ring_end():
            arrive(near(0, 4, *first6), ("zr", 4))
            arrive(near(0, 4, *last6), ("zl", 4))
            along_y(4)

        def cross(dz):
            arrive(near(-1, dz), ("yu", dz))
            send(lambda: near(-1, dz, *first6), lambda: at(dy=1), ("yu2", dz))
            arrive(near(1, dz), ("yd", dz))
            send(lambda: near(1, dz, *last6), lambda: at(dy=-1), ("yd2", dz))
            to_peer(-1, dz)
            to_peer(1, dz)

        def cross_end(dz):
            arrive(near(2, dz, *first6), ("yu2", dz))
            arrive(near(2, dz, *last6), ("yd2", dz))
            to_peer(2, dz)

        events = [(0, 0, start), (0, 1, lambda: factor_start(0))]
        events += [(0, 2 + j, lambda j=j: factor_start(j)) for j in range(1, DESC)]
        events += [(5 * d, 1, lambda d=d: ring(d)) for d in range(1, 4)]
        events += [(17, 1, ring_end)]
        for k, dz in enumerate(Z_ORDER):
            events += [(6 * (k + 1), 2, lambda dz=dz: cross(dz)), (6 * (k + 2), 3, lambda dz=dz: cross_end(dz))]
        events += [(15 * j + 11, 4, lambda j=j: factor_forward(j)) for j in range(DESC)]
        for _, _, event in sorted(events, key=lambda e: e[:2]):
            event()
        for dz in Z_ORDER:
            arrive(far(dz, 0, FAR[0]), ("a", dz))
            arrive(far(dz, FAR[0], COLUMN - FAR[0]), ("b", dz))
        for op in pending:
            op().wait_send()

        @pl.when(y == 0)
        def _():
            copy(sigma_ref.at[pl.ds(12, 4)], far(0, 0, 4), at(dc=1), ("extra",)).wait_send()

    def run_core1():
        piece = {"a": (0, FAR[0]), "b": (FAR[0], COLUMN - FAR[0])}

        def sub(name, which):
            low, count = piece[name]
            at_low, at_count = halves(count)[which]
            return (low + at_low, at_count)

        def around(name):
            send(lambda: far(0, *piece[name]), lambda: at(dz=1), ("zr" + name, 1))
            send(lambda: far(0, *piece[name]), lambda: at(dz=-1), ("zl" + name, 1))
            send(lambda: far(0, *piece[name]), lambda: at(dc=1), (name, 0))

        later = []

        def only(condition, action):
            before = len(pending)

            @pl.when(condition)
            def _():
                action()

            for op in pending[before:]:
                later.append((condition, op))
            del pending[before:]

        def load_own(c):
            if c == 0:
                pieces = [(0, 4, 16)]
            elif c == 1:
                pieces = [(4 * (z // 4), 20, 4), (8 + 4 * (z // 4), 24, 4)]
            elif c == 2:
                pieces = [(2 * (z // 2), 28, 2), (8 + 2 * (z // 2), 30, 2)]
            else:
                pieces = [(2 * (z // 2), 32, 2), (8 + z, 34, 1)]
            ops = [
                pltpu.make_async_copy(
                    sigma_ref.at[pl.ds(src, count)], far(0, dst, count), local_sem.at[2 * DESC + k]
                )
                for k, (src, dst, count) in enumerate(pieces)
            ]
            for op in ops:
                op.start()
            for op in ops:
                op.wait()
            if c == 0:
                arrive(far(0, 0, 4), ("extra",))
            send(lambda: far(0, FAR_AT[c], FAR[c]), lambda: at(dy=1), ("cu",))
            send(lambda: far(0, FAR_AT[c], FAR[c]), lambda: at(dy=-1), ("cd",))

        def from_below(c):
            low, count = halves(FAR[c])[0]
            arrive(far(0, FAR_AT[c], FAR[c]), ("cu",))
            send(lambda: far(0, FAR_AT[c] + low, count), lambda: at(dy=1), ("cu2",))

        def from_above(c):
            low, count = halves(FAR[c])[1]
            arrive(far(0, FAR_AT[c], FAR[c]), ("cd",))
            send(lambda: far(0, FAR_AT[c] + low, count), lambda: at(dy=-1), ("cd2",))

        def from_two(c):
            for (low, count), name in zip(halves(FAR[c]), (("cu2",), ("cd2",))):
                arrive(far(0, FAR_AT[c] + low, count), name)

        def start():
            for c in range(NY):
                only(y == c, lambda c=c: load_own(c))

        def across():
            for c in range(NY):
                only(y == (c + 1) % NY, lambda c=c: from_below(c))
            for c in range(NY):
                only(y == (c - 1) % NY, lambda c=c: from_above(c))
            only(y != 2, lambda: around("a"))

        def across_end():
            for c in range(NY):
                only(y == (c + 2) % NY, lambda c=c: from_two(c))
            only(y == 2, lambda: around("a"))
            around("b")

        def ring(name, d):
            arrive(far(-d, *piece[name]), ("zr" + name, d))
            right = piece[name] if d < 3 else sub(name, 0)
            send(lambda: far(-d, *right), lambda: at(dz=1), ("zr" + name, d + 1))
            arrive(far(d, *piece[name]), ("zl" + name, d))
            left = piece[name] if d < 3 else sub(name, 1)
            send(lambda: far(d, *left), lambda: at(dz=-1), ("zl" + name, d + 1))
            send(lambda: far(-d, *piece[name]), lambda: at(dc=1), (name, -d))
            send(lambda: far(d, *piece[name]), lambda: at(dc=1), (name, d))

        def ring_end(name):
            arrive(far(4, *sub(name, 0)), ("zr" + name, 4))
            arrive(far(4, *sub(name, 1)), ("zl" + name, 4))
            send(lambda: far(4, *piece[name]), lambda: at(dc=1), (name, 4))

        events = [(0, 0, start), (0, 1, lambda: factor_start(0))]
        events += [(0, 2 + j, lambda j=j: factor_start(j)) for j in range(1, DESC)]
        events += [(5, 1, across), (8, 1, across_end)]
        for k, name in enumerate("ab"):
            events += [(11 + 12 * d + 5 * k, 1, lambda d=d, name=name: ring(name, d)) for d in range(1, 4)]
            events += [(54 + k, 1, lambda name=name: ring_end(name))]
        events += [(15 * j + 11, 4, lambda j=j: factor_forward(j)) for j in range(DESC)]
        for _, _, event in sorted(events, key=lambda e: e[:2]):
            event()
        for dy, dz in near_chunks:
            arrive(near(dy, dz), ("n", dy, dz))
        for op in pending:
            op().wait_send()
        for condition, op in later:
            @pl.when(condition)
            def _():
                op().wait_send()

    @pl.when(core == 0)
    def _():
        run_core0()

    pending.clear()

    @pl.when(core == 1)
    def _():
        run_core1()

    pending.clear()

    @pl.loop(0, CH)
    def _(a):
        for b in range(CH):
            lhs[pl.ds(pl.multiple_of(a * Q, Q), Q), pl.ds(b * B, B)] = tiles[idx_ref[a * CH + b]]

    for j in range(DESC):
        factor_done(j)

    for j in range(DESC):
        rhs = full[j].reshape(CH * B, B)

        def step(g, total):
            rows = pl.ds(pl.multiple_of(g * GROUP * Q, Q), GROUP * Q)
            product = jnp.dot(lhs[rows, :], rhs, preferred_element_type=jnp.float32)
            product = product.reshape(GROUP, Q, B)
            blocks = pl.ds(g * GROUP, GROUP)
            cov_ref[j, blocks] = (-product).astype(jnp.bfloat16)
            return total + jnp.sum(own[j, blocks].astype(jnp.float32) * product, axis=(0, 1), keepdims=True)[0]

        total = lax.fori_loop(0, CH // GROUP, step, jnp.zeros((1, B), jnp.float32))
        parts[x, pl.ds(j, 1)] = total + inv_ref[pl.ds(j, 1)]

    for d in range(1, NX):
        send(lambda: parts.at[x], lambda d=d: beside(d), ("vx", d))
    for d in range(1, NX):
        arrive(parts.at[mod(x - d, NX)], ("vx", d))
    mine = table.at[z, y, core]
    mine[...] = (parts[0] + parts[1]) + (parts[2] + parts[3])
    pairs = [(dy, dc) for dy in range(NY) for dc in range(2) if (dy, dc) != (0, 0)]
    for dy, dc in pairs:
        send(lambda: mine, lambda dy=dy, dc=dc: at(dy=dy, dc=dc), ("vy", dy, dc))
    for dy, dc in pairs:
        arrive(table.at[z, mod(y - dy, NY), lax.rem(core + dc, 2)], ("vy", dy, dc))
    for dz in range(1, NZ):
        send(lambda: table.at[z], lambda dz=dz: at(dz=dz), ("vz", dz))
    for dz in range(1, NZ):
        arrive(table.at[mod(z - dz, NZ)], ("vz", dz))
    table_ref[...] = table[...]
    for op in pending:
        op().wait_send()
    assert len(sends) <= SEMS and len(recvs) <= SEMS


SEMS = 240


def tile_slots(subtree):
    upper, middle, lower = subtree // 8, subtree // 4, subtree // 2
    i4 = jnp.arange(4, dtype=jnp.int32)
    i2 = jnp.arange(2, dtype=jnp.int32)
    i8 = jnp.arange(8, dtype=jnp.int32)
    rows = jnp.concatenate([i8, 8 + 4 * upper + i4, 16 + 2 * middle + i2, 24 + lower[None]])
    z = rows % 8
    base = FAR_BASE + z * COLUMN
    near_part = rows[:, None] * NEAR + jnp.arange(NEAR, dtype=jnp.int32)
    first = jnp.where(upper == 0, near_part[:8], jnp.concatenate(
        [near_part[:8, :8], base[:8, None] + i4], axis=1))
    near_part = jnp.concatenate([first, near_part[8:]], axis=0)
    far0 = base[:8, None] + jnp.concatenate([4 + 2 * middle + i2, 12 + lower[None]])
    far1 = base[8:12, None] + jnp.concatenate(
        [20 + 2 * (middle - 2 * upper) + i2, 24 + (lower - 4 * upper)[None]])
    far2 = base[12:14, None] + jnp.concatenate([28 + i2, 30 + (lower - 2 * middle)[None]])
    far3 = base[14:, None] + jnp.arange(32, 35, dtype=jnp.int32)
    far_part = jnp.concatenate([far0, far1, far2, far3], axis=0)
    return jnp.concatenate([near_part, far_part], axis=1).reshape(-1).astype(jnp.int32)


def body(sigma_tiles, panel_factor, panel_mask, inv_diagonal, subtree_of, partition_order):
    leaf = lax.axis_index("leaf")
    x = lax.axis_index("panel")
    slots = tile_slots(subtree_of[leaf])
    mine = (jnp.arange(B) // Q == x)[None, :]
    inverse = jnp.where(mine, jnp.tile(inv_diagonal, (1, NX)), 0.0)
    covariance, table = pl.pallas_call(
        kernel,
        out_shape=(
            jax.ShapeDtypeStruct((DESC, CH, Q, B), jnp.bfloat16),
            jax.ShapeDtypeStruct((NZ, NY, 2, DESC, B), jnp.float32),
        ),
        in_specs=[
            pl.BlockSpec(memory_space=pltpu.SMEM),
            pl.BlockSpec(memory_space=pltpu.SMEM),
            pl.BlockSpec(memory_space=pltpu.VMEM),
            pl.BlockSpec(memory_space=pl.ANY),
            pl.BlockSpec(memory_space=pl.ANY),
        ],
        out_specs=(
            pl.BlockSpec(memory_space=pltpu.VMEM),
            pl.BlockSpec(memory_space=pltpu.VMEM),
        ),
        scratch_shapes=[
            pltpu.VMEM((TILES, Q, B), jnp.bfloat16),
            pltpu.VMEM((CH * Q, CH * B), jnp.bfloat16),
            pltpu.VMEM((DESC, CH, B, B), jnp.bfloat16),
            pltpu.VMEM((DESC, CH, Q, B), jnp.bfloat16),
            pltpu.VMEM((NX, DESC, B), jnp.float32),
            pltpu.VMEM((NZ, NY, 2, DESC, B), jnp.float32),
            pltpu.SemaphoreType.DMA((SEMS,)),
            pltpu.SemaphoreType.DMA((SEMS,)),
            pltpu.SemaphoreType.DMA((2 * DESC + 2,)),
        ],
        compiler_params=pltpu.CompilerParams(
            collective_id=0, has_side_effects=True, vmem_limit_bytes=58 * 1024 * 1024
        ),
    )(slots, panel_mask, inverse, sigma_tiles, panel_factor)
    column = partition_order % B
    block = partition_order // B
    owner, j = block // DESC, block % DESC
    place = (((owner // 2 % NZ * NY + owner // 2 // NZ) * 2 + owner % 2) * DESC + j) * B + column
    variance = jnp.take(table.reshape(-1), place, axis=0)
    return covariance, variance


def solution(mesh):
    placed = (
        P("leaf", "panel", None),
        P("leaf", None, "panel", None),
        P("leaf", None),
        P("leaf", "panel"),
        P(),
        P(("leaf", "panel")),
    )
    return jax.shard_map(
        body,
        mesh=mesh,
        in_specs=placed,
        out_specs=(P("leaf", None, "panel", None), P(("leaf", "panel"))),
        check_vma=False,
    )
```

```python
import jax
import jax.numpy as jnp
from jax import lax
from jax.experimental import pallas as pl
from jax.experimental.pallas import tpu as pltpu
from jax.sharding import PartitionSpec as P

NX, NY, NZ = 4, 4, 8
CH = 15
B = 256
Q = 64
DESC = 4
NEAR = 12
FAR = (20, 8, 4, 3)
FAR_AT = (0, 20, 28, 32)
COLUMN = 35
FAR_BASE = NX * NY * NZ // NX * NEAR
TILES = FAR_BASE + NZ * COLUMN
Z_ORDER = (0, -1, 1, -2, 2, -3, 3, 4)
MESH = pl.DeviceIdType.MESH


def halves(count):
    return (0, (count + 1) // 2), ((count + 1) // 2, count // 2)


def kernel(
    subtree_ref, mask_ref, inv_ref, order_ref, sigma_ref, factor_ref,
    product_ref, variance_ref,
    tiles, lhs, full, own, parts, table,
    send_sem, recv_sem, local_sem,
):
    leaf = lax.axis_index("leaf")
    x = lax.axis_index("panel")
    core = lax.rem(leaf, 2)
    chip = leaf // 2
    y = chip // NZ
    z = lax.rem(chip, NZ)

    def mod(value, size):
        return lax.rem(value + 2 * size, size)

    def at(dy=0, dz=0, dc=0):
        return {"leaf": (mod(y + dy, NY) * NZ + mod(z + dz, NZ)) * 2 + lax.rem(core + dc, 2), "panel": x}

    def beside(dx):
        return {"leaf": leaf, "panel": mod(x + dx, NX)}

    sends = {}
    recvs = {}
    pending = []

    def number(names, name):
        if name not in names:
            names[name] = len(names)
        return names[name]

    def copy(src, dst, device, name):
        return pltpu.make_async_remote_copy(
            src_ref=src, dst_ref=dst,
            send_sem=send_sem.at[number(sends, name)],
            recv_sem=recv_sem.at[number(recvs, name)],
            device_id=device, device_id_type=MESH,
        )

    def send(ref, device, name, src=None):
        def build():
            return copy((src or ref)(), ref(), device(), name)

        build().start()
        pending.append(build)

    def arrive(ref, name):
        copy(ref, ref, beside(1), name).wait_recv()

    for j in range(DESC):
        pltpu.make_async_copy(factor_ref.at[j], own.at[j], local_sem.at[j]).start()

    peers = [beside(1), beside(-1), at(dy=1), at(dy=-1), at(dz=1), at(dz=-1), at(dc=1)]
    barrier = pltpu.get_barrier_semaphore()
    for peer in peers:
        pl.semaphore_signal(barrier, inc=1, device_id=peer, device_id_type=MESH)
    pl.semaphore_wait(barrier, len(peers))

    def quarter(j, dx, low=0, count=CH):
        return full.at[j, pl.ds(low, count), pl.ds(pl.multiple_of(mod(x + dx, NX) * Q, Q), Q)]

    def factor_parts(j):
        first = 8 - j % 2
        return (0, first), (first, CH - first)

    def factor_start(j):
        pltpu.make_async_copy(factor_ref.at[j], own.at[j], local_sem.at[j]).wait()

        @pl.loop(0, CH)
        def _(b):
            own[j, b] = own[j, b] * mask_ref[j, b].astype(jnp.bfloat16)

        send(lambda: quarter(j, 0), lambda: beside(1), ("fr", j), src=lambda: own.at[j])
        send(lambda: quarter(j, 0), lambda: beside(-1), ("fl", j), src=lambda: own.at[j])
        pltpu.make_async_copy(own.at[j], quarter(j, 0), local_sem.at[DESC + j]).start()

    def factor_forward(j):
        right, left = factor_parts(j)
        arrive(quarter(j, -1), ("fr", j))
        send(lambda: quarter(j, -1, *right), lambda: beside(1), ("fr2", j))
        arrive(quarter(j, 1), ("fl", j))
        send(lambda: quarter(j, 1, *left), lambda: beside(-1), ("fl2", j))

    def factor_done(j):
        right, left = factor_parts(j)
        arrive(quarter(j, 2, *right), ("fr2", j))
        arrive(quarter(j, 2, *left), ("fl2", j))
        pltpu.make_async_copy(own.at[j], quarter(j, 0), local_sem.at[DESC + j]).wait()

    def near(dy, dz, low=0, count=NEAR):
        row = mod(y + dy, NY) * NZ + mod(z + dz, NZ)
        return tiles.at[pl.ds(row * NEAR + low, count)]

    def far(dz, low=0, count=COLUMN):
        return tiles.at[pl.ds(FAR_BASE + mod(z + dz, NZ) * COLUMN + low, count)]

    first6, last6 = halves(NEAR)
    near_chunks = [(dy, dz) for dy in range(NY) for dz in Z_ORDER]

    def run_core0():
        def to_peer(dy, dz):
            send(lambda: near(dy, dz), lambda: at(dc=1), ("n", dy % NY, dz))

        def along_y(dz):
            send(lambda: near(0, dz), lambda: at(dy=1), ("yu", dz))
            send(lambda: near(0, dz), lambda: at(dy=-1), ("yd", dz))
            to_peer(0, dz)

        def start():
            @pl.when(y == 0)
            def _():
                ref = far(0, 0, 4)
                copy(sigma_ref.at[pl.ds(12, 4)], ref, at(dc=1), ("extra",)).start()

            upper = jnp.where(y == 0, 0, z // 4)
            one = pltpu.make_async_copy(sigma_ref.at[pl.ds(0, 8)], near(0, 0, 0, 8), local_sem.at[2 * DESC])
            two = pltpu.make_async_copy(
                sigma_ref.at[pl.ds(8 + 4 * upper, 4)], near(0, 0, 8, 4), local_sem.at[2 * DESC + 1]
            )
            one.start()
            two.start()
            one.wait()
            two.wait()
            send(lambda: near(0, 0), lambda: at(dz=1), ("zr", 1))
            send(lambda: near(0, 0), lambda: at(dz=-1), ("zl", 1))
            along_y(0)

        def ring(d):
            arrive(near(0, -d), ("zr", d))
            if d < 3:
                send(lambda: near(0, -d), lambda: at(dz=1), ("zr", d + 1))
            else:
                send(lambda: near(0, -d, *first6), lambda: at(dz=1), ("zr", 4))
            arrive(near(0, d), ("zl", d))
            if d < 3:
                send(lambda: near(0, d), lambda: at(dz=-1), ("zl", d + 1))
            else:
                send(lambda: near(0, d, *last6), lambda: at(dz=-1), ("zl", 4))
            along_y(-d)
            along_y(d)

        def ring_end():
            arrive(near(0, 4, *first6), ("zr", 4))
            arrive(near(0, 4, *last6), ("zl", 4))
            along_y(4)

        def cross(dz):
            arrive(near(-1, dz), ("yu", dz))
            send(lambda: near(-1, dz, *first6), lambda: at(dy=1), ("yu2", dz))
            arrive(near(1, dz), ("yd", dz))
            send(lambda: near(1, dz, *last6), lambda: at(dy=-1), ("yd2", dz))
            to_peer(-1, dz)
            to_peer(1, dz)

        def cross_end(dz):
            arrive(near(2, dz, *first6), ("yu2", dz))
            arrive(near(2, dz, *last6), ("yd2", dz))
            to_peer(2, dz)

        events = [(0, 0, start), (0, 1, lambda: factor_start(0))]
        events += [(0, 2 + j, lambda j=j: factor_start(j)) for j in range(1, DESC)]
        events += [(5 * d, 1, lambda d=d: ring(d)) for d in range(1, 4)]
        events += [(17, 1, ring_end)]
        for k, dz in enumerate(Z_ORDER):
            events += [(6 * (k + 1), 2, lambda dz=dz: cross(dz)), (6 * (k + 2), 3, lambda dz=dz: cross_end(dz))]
        events += [(15 * j + 11, 4, lambda j=j: factor_forward(j)) for j in range(DESC)]
        for _, _, event in sorted(events, key=lambda e: e[:2]):
            event()
        for dz in Z_ORDER:
            arrive(far(dz, 0, FAR[0]), ("a", dz))
            arrive(far(dz, FAR[0], COLUMN - FAR[0]), ("b", dz))
        for op in pending:
            op().wait_send()

        @pl.when(y == 0)
        def _():
            copy(sigma_ref.at[pl.ds(12, 4)], far(0, 0, 4), at(dc=1), ("extra",)).wait_send()

    def run_core1():
        piece = {"a": (0, FAR[0]), "b": (FAR[0], COLUMN - FAR[0])}

        def sub(name, which):
            low, count = piece[name]
            at_low, at_count = halves(count)[which]
            return (low + at_low, at_count)

        def around(name):
            send(lambda: far(0, *piece[name]), lambda: at(dz=1), ("zr" + name, 1))
            send(lambda: far(0, *piece[name]), lambda: at(dz=-1), ("zl" + name, 1))
            send(lambda: far(0, *piece[name]), lambda: at(dc=1), (name, 0))

        later = []

        def only(condition, action):
            before = len(pending)

            @pl.when(condition)
            def _():
                action()

            for op in pending[before:]:
                later.append((condition, op))
            del pending[before:]

        def load_own(c):
            if c == 0:
                pieces = [(0, 4, 16)]
            elif c == 1:
                pieces = [(4 * (z // 4), 20, 4), (8 + 4 * (z // 4), 24, 4)]
            elif c == 2:
                pieces = [(2 * (z // 2), 28, 2), (8 + 2 * (z // 2), 30, 2)]
            else:
                pieces = [(2 * (z // 2), 32, 2), (8 + z, 34, 1)]
            ops = [
                pltpu.make_async_copy(
                    sigma_ref.at[pl.ds(src, count)], far(0, dst, count), local_sem.at[2 * DESC + k]
                )
                for k, (src, dst, count) in enumerate(pieces)
            ]
            for op in ops:
                op.start()
            for op in ops:
                op.wait()
            if c == 0:
                arrive(far(0, 0, 4), ("extra",))
            send(lambda: far(0, FAR_AT[c], FAR[c]), lambda: at(dy=1), ("cu",))
            send(lambda: far(0, FAR_AT[c], FAR[c]), lambda: at(dy=-1), ("cd",))

        def from_below(c):
            low, count = halves(FAR[c])[0]
            arrive(far(0, FAR_AT[c], FAR[c]), ("cu",))
            send(lambda: far(0, FAR_AT[c] + low, count), lambda: at(dy=1), ("cu2",))

        def from_above(c):
            low, count = halves(FAR[c])[1]
            arrive(far(0, FAR_AT[c], FAR[c]), ("cd",))
            send(lambda: far(0, FAR_AT[c] + low, count), lambda: at(dy=-1), ("cd2",))

        def from_two(c):
            for (low, count), name in zip(halves(FAR[c]), (("cu2",), ("cd2",))):
                arrive(far(0, FAR_AT[c] + low, count), name)

        def start():
            for c in range(NY):
                only(y == c, lambda c=c: load_own(c))

        def across():
            for c in range(NY):
                only(y == (c + 1) % NY, lambda c=c: from_below(c))
            for c in range(NY):
                only(y == (c - 1) % NY, lambda c=c: from_above(c))
            only(y != 2, lambda: around("a"))

        def across_end():
            for c in range(NY):
                only(y == (c + 2) % NY, lambda c=c: from_two(c))
            only(y == 2, lambda: around("a"))
            around("b")

        def ring(name, d):
            arrive(far(-d, *piece[name]), ("zr" + name, d))
            right = piece[name] if d < 3 else sub(name, 0)
            send(lambda: far(-d, *right), lambda: at(dz=1), ("zr" + name, d + 1))
            arrive(far(d, *piece[name]), ("zl" + name, d))
            left = piece[name] if d < 3 else sub(name, 1)
            send(lambda: far(d, *left), lambda: at(dz=-1), ("zl" + name, d + 1))
            send(lambda: far(-d, *piece[name]), lambda: at(dc=1), (name, -d))
            send(lambda: far(d, *piece[name]), lambda: at(dc=1), (name, d))

        def ring_end(name):
            arrive(far(4, *sub(name, 0)), ("zr" + name, 4))
            arrive(far(4, *sub(name, 1)), ("zl" + name, 4))
            send(lambda: far(4, *piece[name]), lambda: at(dc=1), (name, 4))

        events = [(0, 0, start), (0, 1, lambda: factor_start(0))]
        events += [(0, 2 + j, lambda j=j: factor_start(j)) for j in range(1, DESC)]
        events += [(5, 1, across), (8, 1, across_end)]
        for k, name in enumerate("ab"):
            events += [(11 + 12 * d + 5 * k, 1, lambda d=d, name=name: ring(name, d)) for d in range(1, 4)]
            events += [(54 + k, 1, lambda name=name: ring_end(name))]
        events += [(15 * j + 11, 4, lambda j=j: factor_forward(j)) for j in range(DESC)]
        for _, _, event in sorted(events, key=lambda e: e[:2]):
            event()
        for dy, dz in near_chunks:
            arrive(near(dy, dz), ("n", dy, dz))
        for op in pending:
            op().wait_send()
        for condition, op in later:
            @pl.when(condition)
            def _():
                op().wait_send()

    @pl.when(core == 0)
    def _():
        run_core0()

    pending.clear()

    @pl.when(core == 1)
    def _():
        run_core1()

    pending.clear()

    subtree = subtree_ref[leaf]
    upper, middle, lower = subtree // 8, subtree // 4, subtree // 2

    def place(a, row, slots):
        for b, slot in enumerate(slots):
            lhs[pl.ds(pl.multiple_of(a * Q, Q), Q), pl.ds(b * B, B)] = tiles[slot]

    def near_slots(row, count):
        return [row * NEAR + k for k in range(count)]

    def column(row):
        return FAR_BASE + lax.rem(row, NZ) * COLUMN

    @pl.loop(0, 8)
    def _(a):
        base = column(a)
        mine = jnp.where(upper == 0, a * NEAR + 8, base)
        slots = near_slots(a, 8) + [mine + k for k in range(4)]
        place(a, a, slots + [base + 4 + 2 * middle, base + 5 + 2 * middle, base + 12 + lower])

    @pl.loop(0, 4)
    def _(i):
        row = 8 + 4 * upper + i
        base = column(row) + FAR_AT[1]
        pair = base + 2 * (middle - 2 * upper)
        place(8 + i, row, near_slots(row, NEAR) + [pair, pair + 1, base + 4 + lower - 4 * upper])

    @pl.loop(0, 2)
    def _(i):
        row = 16 + 2 * middle + i
        base = column(row) + FAR_AT[2]
        place(12 + i, row, near_slots(row, NEAR) + [base, base + 1, base + 2 + lower - 2 * middle])

    row = 24 + lower
    base = column(row) + FAR_AT[3]
    place(14, row, near_slots(row, NEAR) + [base, base + 1, base + 2])

    spot = lax.broadcasted_iota(jnp.int32, (1, HALF), 1) // Q

    @pl.loop(0, DESC)
    def _(j):
        for k in range(DESC):
            @pl.when(j == k)
            def _():
                factor_done(k)

        product = jnp.dot(lhs[...], full[j].reshape(CH * B, B), preferred_element_type=jnp.float32)
        product = product.reshape(CH, Q, B)
        product_ref[j] = product.astype(jnp.bfloat16)
        total = jnp.sum(own[j].astype(jnp.float32) * product, axis=(0, 1), keepdims=True)[0]
        inverse = inv_ref[pl.ds(j, 1)]
        inverse = jnp.concatenate([inverse, inverse], axis=1)
        for half in range(2):
            share = jnp.where(spot + 2 * half == x, inverse, 0.0)
            parts[x, pl.ds(2 * j + half, 1)] = total[:, half * HALF:(half + 1) * HALF] + share

    for d in range(1, NX):
        send(lambda: parts.at[x], lambda d=d: beside(d), ("vx", d))
    for d in range(1, NX):
        arrive(parts.at[mod(x - d, NX)], ("vx", d))
    table[chip, core] = (parts[0] + parts[1]) + (parts[2] + parts[3])
    steps = [(dy, dz) for dz in range(NZ) for dy in range(NY) if (dy, dz) != (0, 0)]
    for dy, dz in steps:
        send(lambda: table.at[chip, core], lambda dy=dy, dz=dz: at(dy=dy, dz=dz), ("vp", dy, dz))
    for dy, dz in steps:
        arrive(table.at[mod(y - dy, NY) * NZ + mod(z - dz, NZ), core], ("vp", dy, dz))
    send(lambda: table.at[:, core], lambda: at(dc=1), ("vc",))
    arrive(table.at[:, lax.rem(core + 1, 2)], ("vc",))

    order = order_ref[...]
    rows = table[...].reshape(NROWS, HALF)
    lane = lax.broadcasted_iota(jnp.int32, (HALF, B), 0)
    pick = jnp.where(lane == order % HALF, 1.0, 0.0).astype(jnp.bfloat16)
    picked = jnp.zeros((NROWS, B), jnp.float32)
    for _ in range(3):
        piece = rows.astype(jnp.bfloat16)
        rows = rows - piece.astype(jnp.float32)
        picked = picked + jnp.dot(piece, pick, preferred_element_type=jnp.float32)
    line = lax.broadcasted_iota(jnp.int32, (NROWS, B), 0)
    variance_ref[...] = jnp.sum(jnp.where(line == order // HALF, picked, 0.0), axis=0, keepdims=True)
    for op in pending:
        op().wait_send()
    assert len(sends) <= SEMS and len(recvs) <= SEMS


SEMS = 240
HALF = B // 2
NROWS = NY * NZ * 2 * 2 * DESC


def body(sigma_tiles, panel_factor, panel_mask, inv_diagonal, subtree_of, partition_order):
    product, variance = pl.pallas_call(
        kernel,
        out_shape=(
            jax.ShapeDtypeStruct((DESC, CH, Q, B), jnp.bfloat16),
            jax.ShapeDtypeStruct((1, B), jnp.float32),
        ),
        in_specs=[
            pl.BlockSpec(memory_space=pltpu.SMEM),
            pl.BlockSpec(memory_space=pltpu.SMEM),
            pl.BlockSpec(memory_space=pltpu.VMEM),
            pl.BlockSpec(memory_space=pltpu.VMEM),
            pl.BlockSpec(memory_space=pl.ANY),
            pl.BlockSpec(memory_space=pl.ANY),
        ],
        out_specs=(
            pl.BlockSpec(memory_space=pltpu.VMEM),
            pl.BlockSpec(memory_space=pltpu.VMEM),
        ),
        scratch_shapes=[
            pltpu.VMEM((TILES, Q, B), jnp.bfloat16),
            pltpu.VMEM((CH * Q, CH * B), jnp.bfloat16),
            pltpu.VMEM((DESC, CH, B, B), jnp.bfloat16),
            pltpu.VMEM((DESC, CH, Q, B), jnp.bfloat16),
            pltpu.VMEM((NX, 2 * DESC, HALF), jnp.float32),
            pltpu.VMEM((NY * NZ, 2, 2 * DESC, HALF), jnp.float32),
            pltpu.SemaphoreType.DMA((SEMS,)),
            pltpu.SemaphoreType.DMA((SEMS,)),
            pltpu.SemaphoreType.DMA((2 * DESC + 2,)),
        ],
        compiler_params=pltpu.CompilerParams(
            collective_id=0, has_side_effects=True, vmem_limit_bytes=58 * 1024 * 1024
        ),
    )(subtree_of, panel_mask, inv_diagonal, partition_order.reshape(1, B), sigma_tiles, panel_factor)
    return -product, variance.reshape(B)


def solution(mesh):
    placed = (
        P("leaf", "panel", None),
        P("leaf", None, "panel", None),
        P("leaf", None),
        P("leaf", "panel"),
        P(),
        P(("leaf", "panel")),
    )
    return jax.shard_map(
        body,
        mesh=mesh,
        in_specs=placed,
        out_specs=(P("leaf", None, "panel", None), P(("leaf", "panel"))),
        check_vma=False,
    )
```

```python
import jax
import jax.numpy as jnp
from jax import lax
from jax.experimental import pallas as pl
from jax.experimental.pallas import tpu as pltpu
from jax.sharding import PartitionSpec as P

NX, NY, NZ = 4, 4, 8
CH = 15
B = 256
Q = 64
DESC = 4
NEAR = 12
FAR = (20, 8, 4, 3)
FAR_AT = (0, 20, 28, 32)
COLUMN = 35
FAR_BASE = NX * NY * NZ // NX * NEAR
TILES = FAR_BASE + NZ * COLUMN
Z_ORDER = (0, -1, 1, -2, 2, -3, 3, 4)
MESH = pl.DeviceIdType.MESH


def halves(count):
    return (0, (count + 1) // 2), ((count + 1) // 2, count // 2)


def kernel(
    subtree_ref, mask_ref, inv_ref, order_ref, sigma_ref, factor_ref,
    product_ref, variance_ref,
    tiles, lhs, full, own, parts, table,
    send_sem, recv_sem, local_sem,
):
    leaf = lax.axis_index("leaf")
    x = lax.axis_index("panel")
    core = lax.rem(leaf, 2)
    chip = leaf // 2
    y = chip // NZ
    z = lax.rem(chip, NZ)

    def mod(value, size):
        return lax.rem(value + 2 * size, size)

    def at(dy=0, dz=0, dc=0):
        return {"leaf": (mod(y + dy, NY) * NZ + mod(z + dz, NZ)) * 2 + lax.rem(core + dc, 2), "panel": x}

    def beside(dx):
        return {"leaf": leaf, "panel": mod(x + dx, NX)}

    sends = {}
    recvs = {}
    pending = []

    def number(names, name):
        if name not in names:
            names[name] = len(names)
        return names[name]

    def copy(src, dst, device, name):
        return pltpu.make_async_remote_copy(
            src_ref=src, dst_ref=dst,
            send_sem=send_sem.at[number(sends, name)],
            recv_sem=recv_sem.at[number(recvs, name)],
            device_id=device, device_id_type=MESH,
        )

    def send(ref, device, name, src=None):
        def build():
            return copy((src or ref)(), ref(), device(), name)

        build().start()
        pending.append(build)

    def arrive(ref, name):
        copy(ref, ref, beside(1), name).wait_recv()

    peers = [beside(1), beside(-1), at(dy=1), at(dy=-1), at(dz=1), at(dz=-1), at(dc=1)]
    barrier = pltpu.get_barrier_semaphore()
    for peer in peers:
        pl.semaphore_signal(barrier, inc=1, device_id=peer, device_id_type=MESH)

    def near(dy, dz, low=0, count=NEAR):
        row = mod(y + dy, NY) * NZ + mod(z + dz, NZ)
        return tiles.at[pl.ds(row * NEAR + low, count)]

    def far(dz, low=0, count=COLUMN):
        return tiles.at[pl.ds(FAR_BASE + mod(z + dz, NZ) * COLUMN + low, count)]

    def own_tiles(pieces):
        ops = [
            pltpu.make_async_copy(sigma_ref.at[pl.ds(src, ref.shape[0])], ref, local_sem.at[2 * DESC + k])
            for k, (src, ref) in enumerate(pieces)
        ]
        for op in ops:
            op.start()
        for op in ops:
            op.wait()

    for j in range(DESC):
        pltpu.make_async_copy(factor_ref.at[j], own.at[j], local_sem.at[j]).start()

    @pl.when(core == 0)
    def _():
        group = jnp.where(y == 0, 0, z // 4)
        own_tiles([(0, near(0, 0, 0, 8)), (8 + 4 * group, near(0, 0, 8, 4))])

    for c in range(NY):
        @pl.when((core == 1) & (y == c))
        def _():
            if c == 0:
                own_tiles([(0, far(0, 4, 16))])
            elif c == 1:
                own_tiles([(4 * (z // 4), far(0, 20, 4)), (8 + 4 * (z // 4), far(0, 24, 4))])
            elif c == 2:
                own_tiles([(2 * (z // 2), far(0, 28, 2)), (8 + 2 * (z // 2), far(0, 30, 2))])
            else:
                own_tiles([(2 * (z // 2), far(0, 32, 2)), (8 + z, far(0, 34, 1))])

    for j in range(DESC):
        pltpu.make_async_copy(factor_ref.at[j], own.at[j], local_sem.at[j]).wait()
        for b in range(CH):
            own[j, b] = own[j, b] * mask_ref[j, b].astype(jnp.bfloat16)
    pl.semaphore_wait(barrier, len(peers))

    def quarter(j, dx, low=0, count=CH):
        return full.at[j, pl.ds(low, count), pl.ds(pl.multiple_of(mod(x + dx, NX) * Q, Q), Q)]

    def factor_parts(j):
        first = 8 - j % 2
        return (0, first), (first, CH - first)

    def factor_start(j):
        send(lambda: quarter(j, 0), lambda: beside(1), ("fr", j), src=lambda: own.at[j])
        send(lambda: quarter(j, 0), lambda: beside(-1), ("fl", j), src=lambda: own.at[j])
        pltpu.make_async_copy(own.at[j], quarter(j, 0), local_sem.at[DESC + j]).start()

    def factor_forward(j):
        right, left = factor_parts(j)
        arrive(quarter(j, -1), ("fr", j))
        send(lambda: quarter(j, -1, *right), lambda: beside(1), ("fr2", j))
        arrive(quarter(j, 1), ("fl", j))
        send(lambda: quarter(j, 1, *left), lambda: beside(-1), ("fl2", j))

    def factor_done(j):
        right, left = factor_parts(j)
        arrive(quarter(j, 2, *right), ("fr2", j))
        arrive(quarter(j, 2, *left), ("fl2", j))
        pltpu.make_async_copy(own.at[j], quarter(j, 0), local_sem.at[DESC + j]).wait()

    first6, last6 = halves(NEAR)
    near_chunks = [(dy, dz) for dy in range(NY) for dz in Z_ORDER]

    def run_core0():
        def to_peer(dy, dz):
            send(lambda: near(dy, dz), lambda: at(dc=1), ("n", dy % NY, dz))

        def along_y(dz):
            send(lambda: near(0, dz), lambda: at(dy=1), ("yu", dz))
            send(lambda: near(0, dz), lambda: at(dy=-1), ("yd", dz))
            to_peer(0, dz)

        def start():
            @pl.when(y == 0)
            def _():
                ref = far(0, 0, 4)
                copy(sigma_ref.at[pl.ds(12, 4)], ref, at(dc=1), ("extra",)).start()

            send(lambda: near(0, 0), lambda: at(dz=1), ("zr", 1))
            send(lambda: near(0, 0), lambda: at(dz=-1), ("zl", 1))
            along_y(0)

        def ring(d):
            arrive(near(0, -d), ("zr", d))
            if d < 3:
                send(lambda: near(0, -d), lambda: at(dz=1), ("zr", d + 1))
            else:
                send(lambda: near(0, -d, *first6), lambda: at(dz=1), ("zr", 4))
            arrive(near(0, d), ("zl", d))
            if d < 3:
                send(lambda: near(0, d), lambda: at(dz=-1), ("zl", d + 1))
            else:
                send(lambda: near(0, d, *last6), lambda: at(dz=-1), ("zl", 4))
            along_y(-d)
            along_y(d)

        def ring_end():
            arrive(near(0, 4, *first6), ("zr", 4))
            arrive(near(0, 4, *last6), ("zl", 4))
            along_y(4)

        def cross(dz):
            arrive(near(-1, dz), ("yu", dz))
            send(lambda: near(-1, dz, *first6), lambda: at(dy=1), ("yu2", dz))
            arrive(near(1, dz), ("yd", dz))
            send(lambda: near(1, dz, *last6), lambda: at(dy=-1), ("yd2", dz))
            to_peer(-1, dz)
            to_peer(1, dz)

        def cross_end(dz):
            arrive(near(2, dz, *first6), ("yu2", dz))
            arrive(near(2, dz, *last6), ("yd2", dz))
            to_peer(2, dz)

        events = [(0, 0, lambda: factor_start(0)), (0, 1, start)]
        events += [(0, 2 + j, lambda j=j: factor_start(j)) for j in range(1, DESC)]
        events += [(5 * d, 1, lambda d=d: ring(d)) for d in range(1, 4)]
        events += [(17, 1, ring_end)]
        for k, dz in enumerate(Z_ORDER):
            events += [(6 * (k + 1), 2, lambda dz=dz: cross(dz)), (6 * (k + 2), 3, lambda dz=dz: cross_end(dz))]
        events += [(11 * j + 15, 4, lambda j=j: factor_forward(j)) for j in range(DESC)]
        for _, _, event in sorted(events, key=lambda e: e[:2]):
            event()
        for dz in Z_ORDER:
            for which in range(2):
                low, count = halves(FAR[0])[which]
                arrive(far(dz, low, count), ("p", "0" + "ab"[which], dz))
            for c in range(1, NY):
                arrive(far(dz, FAR_AT[c], FAR[c]), ("p", str(c), dz))

    def finish_core0():
        for op in sent[0]:
            op().wait_send()

        @pl.when(y == 0)
        def _():
            copy(sigma_ref.at[pl.ds(12, 4)], far(0, 0, 4), at(dc=1), ("extra",)).wait_send()

    later = []

    def run_core1():
        def part(c, which):
            low, count = halves(FAR[c])[which]
            return (FAR_AT[c] + low, count)

        def only(row, action):
            before = len(pending)

            @pl.when(y == row)
            def _():
                action()

            for op in pending[before:]:
                later.append((row, op))
            del pending[before:]

        def around(c, which):
            low, count = part(c, which) if c == 0 else (FAR_AT[c], FAR[c])
            name = piece_name(c, which)
            send(lambda: far(0, low, count), lambda: at(dz=1), ("zr" + name, 1))
            send(lambda: far(0, low, count), lambda: at(dz=-1), ("zl" + name, 1))
            send(lambda: far(0, low, count), lambda: at(dc=1), ("p", name, 0))

        def piece_name(c, which):
            return "0" + "ab"[which] if c == 0 else str(c)

        def across_send(c, which, up):
            send(lambda: far(0, *part(c, which)), lambda: at(dy=1 if up else -1), ("c", up, which))

        def load_own(c):
            across_send(c, 1, False)
            if c == 0:
                around(0, 1)
                arrive(far(0, 0, 4), ("extra",))
            across_send(c, 0, True)
            across_send(c, 0, False)
            across_send(c, 1, True)
            around(c, 0)

        def from_below(c):
            arrive(far(0, *part(c, 0)), ("c", True, 0))
            send(lambda: far(0, *part(c, 0)), lambda: at(dy=1), ("c2", 0))

        def from_above(c):
            arrive(far(0, *part(c, 1)), ("c", False, 1))
            send(lambda: far(0, *part(c, 1)), lambda: at(dy=-1), ("c2", 1))

        def rest_below(c):
            if c == 0:
                around(0, 0)
            arrive(far(0, *part(c, 1)), ("c", True, 1))
            around(c, 1)

        def rest_above(c):
            if c == 0:
                around(0, 1)
            arrive(far(0, *part(c, 0)), ("c", False, 0))
            around(c, 0)

        def from_two(c):
            arrive(far(0, *part(c, 1)), ("c2", 1))
            if c == 0:
                around(0, 1)
            arrive(far(0, *part(c, 0)), ("c2", 0))
            around(c, 0)

        def start():
            for c in range(NY):
                only(c, lambda c=c: load_own(c))

        def across():
            for action, dy in ((from_below, 1), (from_above, -1), (rest_below, 1), (rest_above, -1)):
                for c in range(NY):
                    only((c + dy) % NY, lambda c=c, action=action: action(c))

        def across_end():
            for c in range(NY):
                only((c + 2) % NY, lambda c=c: from_two(c))

        rings = {
            "0a": (part(0, 0), part(0, 0), None),
            "0b": (part(0, 1), None, part(0, 1)),
        }
        for c in range(1, NY):
            rings[str(c)] = ((FAR_AT[c], FAR[c]), part(c, 0), part(c, 1))

        def ring(name, d):
            whole, right, left = rings[name]
            arrive(far(-d, *whole), ("zr" + name, d))
            right = whole if d < 3 else right
            if right:
                send(lambda: far(-d, *right), lambda: at(dz=1), ("zr" + name, d + 1))
            arrive(far(d, *whole), ("zl" + name, d))
            left = whole if d < 3 else left
            if left:
                send(lambda: far(d, *left), lambda: at(dz=-1), ("zl" + name, d + 1))
            send(lambda: far(-d, *whole), lambda: at(dc=1), ("p", name, -d))
            send(lambda: far(d, *whole), lambda: at(dc=1), ("p", name, d))

        def ring_end(name):
            whole, right, left = rings[name]
            if right:
                arrive(far(4, *right), ("zr" + name, 4))
            if left:
                arrive(far(4, *left), ("zl" + name, 4))
            send(lambda: far(4, *whole), lambda: at(dc=1), ("p", name, 4))

        events = [(0, 0, lambda: factor_start(0)), (0, 1, start)]
        events += [(0, 2 + j, lambda j=j: factor_start(j)) for j in range(1, DESC)]
        events += [(5, 1, across), (8, 1, across_end)]
        for k, name in enumerate(RING_ORDER):
            events += [(11 + 12 * d + 2 * k, 1, lambda d=d, name=name: ring(name, d)) for d in range(1, 4)]
            events += [(59 + k, 1, lambda name=name: ring_end(name))]
        events += [(11 * j + 15, 4, lambda j=j: factor_forward(j)) for j in range(DESC)]
        for _, _, event in sorted(events, key=lambda e: e[:2]):
            event()
        for dy, dz in near_chunks:
            arrive(near(dy, dz), ("n", dy, dz))

    def finish_core1():
        for op in sent[1]:
            op().wait_send()
        for row, op in later:
            @pl.when(y == row)
            def _():
                op().wait_send()

    @pl.when(core == 0)
    def _():
        run_core0()

    sent = [list(pending)]
    pending.clear()

    @pl.when(core == 1)
    def _():
        run_core1()

    sent.append(list(pending))
    pending.clear()

    subtree = subtree_ref[leaf]
    upper, middle, lower = subtree // 8, subtree // 4, subtree // 2

    def place(a, row, slots):
        for b, slot in enumerate(slots):
            lhs[pl.ds(pl.multiple_of(a * Q, Q), Q), pl.ds(b * B, B)] = tiles[slot]

    def near_slots(row, count):
        return [row * NEAR + k for k in range(count)]

    def column(row):
        return FAR_BASE + lax.rem(row, NZ) * COLUMN

    @pl.loop(0, 8)
    def _(a):
        base = column(a)
        mine = jnp.where(upper == 0, a * NEAR + 8, base)
        slots = near_slots(a, 8) + [mine + k for k in range(4)]
        place(a, a, slots + [base + 4 + 2 * middle, base + 5 + 2 * middle, base + 12 + lower])

    @pl.loop(0, 4)
    def _(i):
        row = 8 + 4 * upper + i
        base = column(row) + FAR_AT[1]
        pair = base + 2 * (middle - 2 * upper)
        place(8 + i, row, near_slots(row, NEAR) + [pair, pair + 1, base + 4 + lower - 4 * upper])

    @pl.loop(0, 2)
    def _(i):
        row = 16 + 2 * middle + i
        base = column(row) + FAR_AT[2]
        place(12 + i, row, near_slots(row, NEAR) + [base, base + 1, base + 2 + lower - 2 * middle])

    row = 24 + lower
    base = column(row) + FAR_AT[3]
    place(14, row, near_slots(row, NEAR) + [base, base + 1, base + 2])

    spot = lax.broadcasted_iota(jnp.int32, (1, HALF), 1) // Q

    @pl.loop(0, DESC)
    def _(j):
        for k in range(DESC):
            @pl.when(j == k)
            def _():
                factor_done(k)

        product = jnp.dot(lhs[...], full[j].reshape(CH * B, B), preferred_element_type=jnp.float32)
        product = product.reshape(CH, Q, B)
        product_ref[j] = product.astype(jnp.bfloat16)
        total = jnp.sum(own[j].astype(jnp.float32) * product, axis=(0, 1), keepdims=True)[0]
        inverse = inv_ref[pl.ds(j, 1)]
        inverse = jnp.concatenate([inverse, inverse], axis=1)
        for half in range(2):
            share = jnp.where(spot + 2 * half == x, inverse, 0.0)
            parts[x, pl.ds(2 * j + half, 1)] = total[:, half * HALF:(half + 1) * HALF] + share

    for d in range(1, NX):
        send(lambda: parts.at[x], lambda d=d: beside(d), ("vx", d))
    for d in range(1, NX):
        arrive(parts.at[mod(x - d, NX)], ("vx", d))
    table[chip, core] = (parts[0] + parts[1]) + (parts[2] + parts[3])
    steps = [(dy, dz) for dz in range(NZ) for dy in range(NY) if (dy, dz) != (0, 0)]
    for dy, dz in steps:
        send(lambda: table.at[chip, core], lambda dy=dy, dz=dz: at(dy=dy, dz=dz), ("vp", dy, dz))
    for dy, dz in steps:
        arrive(table.at[mod(y - dy, NY) * NZ + mod(z - dz, NZ), core], ("vp", dy, dz))
    send(lambda: table.at[:, core], lambda: at(dc=1), ("vc",))
    arrive(table.at[:, lax.rem(core + 1, 2)], ("vc",))

    order = order_ref[...]
    rows = table[...].reshape(NROWS, HALF)
    lane = lax.broadcasted_iota(jnp.int32, (HALF, B), 0)
    pick = jnp.where(lane == order % HALF, 1.0, 0.0).astype(jnp.bfloat16)
    picked = jnp.zeros((NROWS, B), jnp.float32)
    for _ in range(3):
        piece = rows.astype(jnp.bfloat16)
        rows = rows - piece.astype(jnp.float32)
        picked = picked + jnp.dot(piece, pick, preferred_element_type=jnp.float32)
    line = lax.broadcasted_iota(jnp.int32, (NROWS, B), 0)
    variance_ref[...] = jnp.sum(jnp.where(line == order // HALF, picked, 0.0), axis=0, keepdims=True)
    for op in pending:
        op().wait_send()

    @pl.when(core == 0)
    def _():
        finish_core0()

    @pl.when(core == 1)
    def _():
        finish_core1()

    assert len(sends) <= SEMS and len(recvs) <= SEMS


SEMS = 240
RING_ORDER = ("1", "2", "3", "0b", "0a")
HALF = B // 2
NROWS = NY * NZ * 2 * 2 * DESC


def body(sigma_tiles, panel_factor, panel_mask, inv_diagonal, subtree_of, partition_order):
    product, variance = pl.pallas_call(
        kernel,
        out_shape=(
            jax.ShapeDtypeStruct((DESC, CH, Q, B), jnp.bfloat16),
            jax.ShapeDtypeStruct((1, B), jnp.float32),
        ),
        in_specs=[
            pl.BlockSpec(memory_space=pltpu.SMEM),
            pl.BlockSpec(memory_space=pltpu.SMEM),
            pl.BlockSpec(memory_space=pltpu.VMEM),
            pl.BlockSpec(memory_space=pltpu.VMEM),
            pl.BlockSpec(memory_space=pl.ANY),
            pl.BlockSpec(memory_space=pl.ANY),
        ],
        out_specs=(
            pl.BlockSpec(memory_space=pltpu.VMEM),
            pl.BlockSpec(memory_space=pltpu.VMEM),
        ),
        scratch_shapes=[
            pltpu.VMEM((TILES, Q, B), jnp.bfloat16),
            pltpu.VMEM((CH * Q, CH * B), jnp.bfloat16),
            pltpu.VMEM((DESC, CH, B, B), jnp.bfloat16),
            pltpu.VMEM((DESC, CH, Q, B), jnp.bfloat16),
            pltpu.VMEM((NX, 2 * DESC, HALF), jnp.float32),
            pltpu.VMEM((NY * NZ, 2, 2 * DESC, HALF), jnp.float32),
            pltpu.SemaphoreType.DMA((SEMS,)),
            pltpu.SemaphoreType.DMA((SEMS,)),
            pltpu.SemaphoreType.DMA((2 * DESC + 2,)),
        ],
        compiler_params=pltpu.CompilerParams(
            collective_id=0, has_side_effects=True, vmem_limit_bytes=44 * 1024 * 1024
        ),
    )(subtree_of, panel_mask, inv_diagonal, partition_order.reshape(1, B), sigma_tiles, panel_factor)
    return -product, variance.reshape(B)


def solution(mesh):
    placed = (
        P("leaf", "panel", None),
        P("leaf", None, "panel", None),
        P("leaf", None),
        P("leaf", "panel"),
        P(),
        P(("leaf", "panel")),
    )
    return jax.shard_map(
        body,
        mesh=mesh,
        in_specs=placed,
        out_specs=(P("leaf", None, "panel", None), P(("leaf", "panel"))),
        check_vma=False,
    )
```

```python
import jax
import jax.numpy as jnp
from jax import lax
from jax.experimental import pallas as pl
from jax.experimental.pallas import tpu as pltpu
from jax.sharding import PartitionSpec as P

NX, NY, NZ = 4, 4, 8
CH = 15
B = 256
Q = 64
DESC = 4
NEAR = 12
FAR = (20, 8, 4, 3)
FAR_AT = (0, 20, 28, 32)
COLUMN = 35
FAR_BASE = NX * NY * NZ // NX * NEAR
TILES = FAR_BASE + NZ * COLUMN
Z_ORDER = (0, -1, 1, -2, 2, -3, 3, 4)
MESH = pl.DeviceIdType.MESH


def halves(count):
    return (0, (count + 1) // 2), ((count + 1) // 2, count // 2)


def kernel(
    subtree_hbm, mask_hbm, inv_hbm, order_hbm, sigma_ref, factor_ref,
    product_ref, variance_ref,
    tiles, lhs, full, own, rounded, parts, table,
    subtree_ref, mask_ref, inv_ref, order_ref,
    send_sem, recv_sem, local_sem, small_sem,
):
    leaf = lax.axis_index("leaf")
    x = lax.axis_index("panel")
    core = lax.rem(leaf, 2)
    chip = leaf // 2
    y = chip // NZ
    z = lax.rem(chip, NZ)

    def mod(value, size):
        return lax.rem(value + 2 * size, size)

    def at(dy=0, dz=0, dc=0):
        return {"leaf": (mod(y + dy, NY) * NZ + mod(z + dz, NZ)) * 2 + lax.rem(core + dc, 2), "panel": x}

    def beside(dx):
        return {"leaf": leaf, "panel": mod(x + dx, NX)}

    sends = {}
    recvs = {}
    pending = []

    def number(names, name):
        if name not in names:
            names[name] = len(names)
        return names[name]

    def copy(src, dst, device, name):
        return pltpu.make_async_remote_copy(
            src_ref=src, dst_ref=dst,
            send_sem=send_sem.at[number(sends, name)],
            recv_sem=recv_sem.at[number(recvs, name)],
            device_id=device, device_id_type=MESH,
        )

    def send(ref, device, name, src=None):
        def build():
            return copy((src or ref)(), ref(), device(), name)

        build().start()
        pending.append(build)

    def arrive(ref, name):
        copy(ref, ref, beside(1), name).wait_recv()

    peers = [beside(1), beside(-1), at(dy=1), at(dy=-1), at(dz=1), at(dz=-1), at(dc=1)]
    barrier = pltpu.get_barrier_semaphore()
    for peer in peers:
        pl.semaphore_signal(barrier, inc=1, device_id=peer, device_id_type=MESH)

    def near(dy, dz, low=0, count=NEAR):
        row = mod(y + dy, NY) * NZ + mod(z + dz, NZ)
        return tiles.at[pl.ds(row * NEAR + low, count)]

    def far(dz, low=0, count=COLUMN):
        return tiles.at[pl.ds(FAR_BASE + mod(z + dz, NZ) * COLUMN + low, count)]

    def own_tiles(pieces):
        ops = [
            pltpu.make_async_copy(sigma_ref.at[pl.ds(src, ref.shape[0])], ref, local_sem.at[2 * DESC + k])
            for k, (src, ref) in enumerate(pieces)
        ]
        for op in ops:
            op.start()
        for op in ops:
            op.wait()

    for j in range(DESC):
        pltpu.make_async_copy(factor_ref.at[j], own.at[j], local_sem.at[j]).start()

    small = [
        pltpu.make_async_copy(src, dst, small_sem.at[k])
        for k, (src, dst) in enumerate((
            (mask_hbm, mask_ref), (subtree_hbm, subtree_ref), (inv_hbm, inv_ref), (order_hbm, order_ref),
        ))
    ]
    for op in small:
        op.start()

    @pl.when(core == 0)
    def _():
        group = jnp.where(y == 0, 0, z // 4)
        own_tiles([(0, near(0, 0, 0, 8)), (8 + 4 * group, near(0, 0, 8, 4))])

    for c in range(NY):
        @pl.when((core == 1) & (y == c))
        def _():
            if c == 0:
                own_tiles([(0, far(0, 4, 16))])
            elif c == 1:
                own_tiles([(4 * (z // 4), far(0, 20, 4)), (8 + 4 * (z // 4), far(0, 24, 4))])
            elif c == 2:
                own_tiles([(2 * (z // 2), far(0, 28, 2)), (8 + 2 * (z // 2), far(0, 30, 2))])
            else:
                own_tiles([(2 * (z // 2), far(0, 32, 2)), (8 + z, far(0, 34, 1))])

    for op in small:
        op.wait()
    for j in range(DESC):
        pltpu.make_async_copy(factor_ref.at[j], own.at[j], local_sem.at[j]).wait()
        for b in range(CH):
            own[j, b] = own[j, b] * mask_ref[j, b].astype(jnp.bfloat16)
    pl.semaphore_wait(barrier, len(peers))

    def quarter(j, dx, low=0, count=CH):
        return full.at[j, pl.ds(low, count), pl.ds(pl.multiple_of(mod(x + dx, NX) * Q, Q), Q)]

    def factor_parts(j):
        first = 8 - j % 2
        return (0, first), (first, CH - first)

    def factor_start(j):
        send(lambda: quarter(j, 0), lambda: beside(1), ("fr", j), src=lambda: own.at[j])
        send(lambda: quarter(j, 0), lambda: beside(-1), ("fl", j), src=lambda: own.at[j])
        pltpu.make_async_copy(own.at[j], quarter(j, 0), local_sem.at[DESC + j]).start()

    def factor_forward(j):
        right, left = factor_parts(j)
        arrive(quarter(j, -1), ("fr", j))
        send(lambda: quarter(j, -1, *right), lambda: beside(1), ("fr2", j))
        arrive(quarter(j, 1), ("fl", j))
        send(lambda: quarter(j, 1, *left), lambda: beside(-1), ("fl2", j))

    def factor_done(j):
        right, left = factor_parts(j)
        arrive(quarter(j, 2, *right), ("fr2", j))
        arrive(quarter(j, 2, *left), ("fl2", j))
        pltpu.make_async_copy(own.at[j], quarter(j, 0), local_sem.at[DESC + j]).wait()

    first6, last6 = halves(NEAR)
    near_chunks = [(dy, dz) for dy in range(NY) for dz in Z_ORDER]

    def run_core0():
        def to_peer(dy, dz):
            send(lambda: near(dy, dz), lambda: at(dc=1), ("n", dy % NY, dz))

        def along_y(dz):
            send(lambda: near(0, dz), lambda: at(dy=1), ("yu", dz))
            send(lambda: near(0, dz), lambda: at(dy=-1), ("yd", dz))
            to_peer(0, dz)

        def start():
            @pl.when(y == 0)
            def _():
                ref = far(0, 0, 4)
                copy(sigma_ref.at[pl.ds(12, 4)], ref, at(dc=1), ("extra",)).start()

            send(lambda: near(0, 0), lambda: at(dz=1), ("zr", 1))
            send(lambda: near(0, 0), lambda: at(dz=-1), ("zl", 1))
            along_y(0)

        def ring(d):
            arrive(near(0, -d), ("zr", d))
            if d < 3:
                send(lambda: near(0, -d), lambda: at(dz=1), ("zr", d + 1))
            else:
                send(lambda: near(0, -d, *first6), lambda: at(dz=1), ("zr", 4))
            arrive(near(0, d), ("zl", d))
            if d < 3:
                send(lambda: near(0, d), lambda: at(dz=-1), ("zl", d + 1))
            else:
                send(lambda: near(0, d, *last6), lambda: at(dz=-1), ("zl", 4))
            along_y(-d)
            along_y(d)

        def ring_end():
            arrive(near(0, 4, *first6), ("zr", 4))
            arrive(near(0, 4, *last6), ("zl", 4))
            along_y(4)

        def cross(dz):
            arrive(near(-1, dz), ("yu", dz))
            send(lambda: near(-1, dz, *first6), lambda: at(dy=1), ("yu2", dz))
            arrive(near(1, dz), ("yd", dz))
            send(lambda: near(1, dz, *last6), lambda: at(dy=-1), ("yd2", dz))
            to_peer(-1, dz)
            to_peer(1, dz)

        def cross_end(dz):
            arrive(near(2, dz, *first6), ("yu2", dz))
            arrive(near(2, dz, *last6), ("yd2", dz))
            to_peer(2, dz)

        events = [(0, 0, lambda: factor_start(0)), (0, 1, start)]
        events += [(0, 2 + j, lambda j=j: factor_start(j)) for j in range(1, DESC)]
        events += [(5 * d, 1, lambda d=d: ring(d)) for d in range(1, 4)]
        events += [(17, 1, ring_end)]
        for k, dz in enumerate(Z_ORDER):
            events += [(6 * (k + 1), 2, lambda dz=dz: cross(dz)), (6 * (k + 2), 3, lambda dz=dz: cross_end(dz))]
        events += [(11 * j + 15, 4, lambda j=j: factor_forward(j)) for j in range(DESC)]
        for _, _, event in sorted(events, key=lambda e: e[:2]):
            event()
        for dz in Z_ORDER:
            for which in range(2):
                low, count = halves(FAR[0])[which]
                arrive(far(dz, low, count), ("p", "0" + "ab"[which], dz))
            for c in range(1, NY):
                arrive(far(dz, FAR_AT[c], FAR[c]), ("p", str(c), dz))

    def finish_core0():
        for op in sent[0]:
            op().wait_send()

        @pl.when(y == 0)
        def _():
            copy(sigma_ref.at[pl.ds(12, 4)], far(0, 0, 4), at(dc=1), ("extra",)).wait_send()

    later = []

    def run_core1():
        def part(c, which):
            low, count = halves(FAR[c])[which]
            return (FAR_AT[c] + low, count)

        def only(row, action):
            before = len(pending)

            @pl.when(y == row)
            def _():
                action()

            for op in pending[before:]:
                later.append((row, op))
            del pending[before:]

        def around(c, which):
            low, count = part(c, which) if c == 0 else (FAR_AT[c], FAR[c])
            name = piece_name(c, which)
            send(lambda: far(0, low, count), lambda: at(dz=1), ("zr" + name, 1))
            send(lambda: far(0, low, count), lambda: at(dz=-1), ("zl" + name, 1))
            send(lambda: far(0, low, count), lambda: at(dc=1), ("p", name, 0))

        def piece_name(c, which):
            return "0" + "ab"[which] if c == 0 else str(c)

        def across_send(c, which, up):
            send(lambda: far(0, *part(c, which)), lambda: at(dy=1 if up else -1), ("c", up, which))

        def load_own(c):
            across_send(c, 1, False)
            if c == 0:
                around(0, 1)
                arrive(far(0, 0, 4), ("extra",))
            across_send(c, 0, True)
            across_send(c, 0, False)
            across_send(c, 1, True)
            around(c, 0)

        def from_below(c):
            arrive(far(0, *part(c, 0)), ("c", True, 0))
            send(lambda: far(0, *part(c, 0)), lambda: at(dy=1), ("c2", 0))

        def from_above(c):
            arrive(far(0, *part(c, 1)), ("c", False, 1))
            send(lambda: far(0, *part(c, 1)), lambda: at(dy=-1), ("c2", 1))

        def rest_below(c):
            if c == 0:
                around(0, 0)
            arrive(far(0, *part(c, 1)), ("c", True, 1))
            around(c, 1)

        def rest_above(c):
            if c == 0:
                around(0, 1)
            arrive(far(0, *part(c, 0)), ("c", False, 0))
            around(c, 0)

        def from_two(c):
            arrive(far(0, *part(c, 1)), ("c2", 1))
            if c == 0:
                around(0, 1)
            arrive(far(0, *part(c, 0)), ("c2", 0))
            around(c, 0)

        def start():
            for c in range(NY):
                only(c, lambda c=c: load_own(c))

        def across():
            for action, dy in ((from_below, 1), (from_above, -1), (rest_below, 1), (rest_above, -1)):
                for c in range(NY):
                    only((c + dy) % NY, lambda c=c, action=action: action(c))

        def across_end():
            for c in range(NY):
                only((c + 2) % NY, lambda c=c: from_two(c))

        rings = {
            "0a": (part(0, 0), part(0, 0), None),
            "0b": (part(0, 1), None, part(0, 1)),
        }
        for c in range(1, NY):
            rings[str(c)] = ((FAR_AT[c], FAR[c]), part(c, 0), part(c, 1))

        def ring(name, d):
            whole, right, left = rings[name]
            arrive(far(-d, *whole), ("zr" + name, d))
            right = whole if d < 3 else right
            if right:
                send(lambda: far(-d, *right), lambda: at(dz=1), ("zr" + name, d + 1))
            arrive(far(d, *whole), ("zl" + name, d))
            left = whole if d < 3 else left
            if left:
                send(lambda: far(d, *left), lambda: at(dz=-1), ("zl" + name, d + 1))
            send(lambda: far(-d, *whole), lambda: at(dc=1), ("p", name, -d))
            send(lambda: far(d, *whole), lambda: at(dc=1), ("p", name, d))

        def ring_end(name):
            whole, right, left = rings[name]
            if right:
                arrive(far(4, *right), ("zr" + name, 4))
            if left:
                arrive(far(4, *left), ("zl" + name, 4))
            send(lambda: far(4, *whole), lambda: at(dc=1), ("p", name, 4))

        events = [(0, 0, lambda: factor_start(0)), (0, 1, start)]
        events += [(0, 2 + j, lambda j=j: factor_start(j)) for j in range(1, DESC)]
        events += [(5, 1, across), (8, 1, across_end)]
        for k, name in enumerate(RING_ORDER):
            events += [(11 + 12 * d + 2 * k, 1, lambda d=d, name=name: ring(name, d)) for d in range(1, 4)]
            events += [(59 + k, 1, lambda name=name: ring_end(name))]
        events += [(11 * j + 15, 4, lambda j=j: factor_forward(j)) for j in range(DESC)]
        for _, _, event in sorted(events, key=lambda e: e[:2]):
            event()
        for dy, dz in near_chunks:
            arrive(near(dy, dz), ("n", dy, dz))

    def finish_core1():
        for op in sent[1]:
            op().wait_send()
        for row, op in later:
            @pl.when(y == row)
            def _():
                op().wait_send()

    @pl.when(core == 0)
    def _():
        run_core0()

    sent = [list(pending)]
    pending.clear()

    @pl.when(core == 1)
    def _():
        run_core1()

    sent.append(list(pending))
    pending.clear()

    subtree = subtree_ref[leaf]
    upper, middle, lower = subtree // 8, subtree // 4, subtree // 2

    def place(a, row, slots):
        for b, slot in enumerate(slots):
            lhs[pl.ds(pl.multiple_of(a * Q, Q), Q), pl.ds(b * B, B)] = tiles[slot]

    def near_slots(row, count):
        return [row * NEAR + k for k in range(count)]

    def column(row):
        return FAR_BASE + lax.rem(row, NZ) * COLUMN

    @pl.loop(0, 8)
    def _(a):
        base = column(a)
        mine = jnp.where(upper == 0, a * NEAR + 8, base)
        slots = near_slots(a, 8) + [mine + k for k in range(4)]
        place(a, a, slots + [base + 4 + 2 * middle, base + 5 + 2 * middle, base + 12 + lower])

    @pl.loop(0, 4)
    def _(i):
        row = 8 + 4 * upper + i
        base = column(row) + FAR_AT[1]
        pair = base + 2 * (middle - 2 * upper)
        place(8 + i, row, near_slots(row, NEAR) + [pair, pair + 1, base + 4 + lower - 4 * upper])

    @pl.loop(0, 2)
    def _(i):
        row = 16 + 2 * middle + i
        base = column(row) + FAR_AT[2]
        place(12 + i, row, near_slots(row, NEAR) + [base, base + 1, base + 2 + lower - 2 * middle])

    row = 24 + lower
    base = column(row) + FAR_AT[3]
    place(14, row, near_slots(row, NEAR) + [base, base + 1, base + 2])

    spot = lax.broadcasted_iota(jnp.int32, (1, HALF), 1) // Q

    @pl.loop(0, DESC)
    def _(j):
        for k in range(DESC):
            @pl.when(j == k)
            def _():
                factor_done(k)

        product = jnp.dot(lhs[...], full[j].reshape(CH * B, B), preferred_element_type=jnp.float32)
        product = product.reshape(CH, Q, B)
        rounded[j] = product.astype(jnp.bfloat16)
        pltpu.make_async_copy(rounded.at[j], product_ref.at[j], local_sem.at[j]).start()
        total = jnp.sum(own[j].astype(jnp.float32) * product, axis=(0, 1), keepdims=True)[0]
        inverse = inv_ref[pl.ds(j, 1)]
        inverse = jnp.concatenate([inverse, inverse], axis=1)
        for half in range(2):
            share = jnp.where(spot + 2 * half == x, inverse, 0.0)
            parts[x, pl.ds(2 * j + half, 1)] = total[:, half * HALF:(half + 1) * HALF] + share

    for d in range(1, NX):
        send(lambda: parts.at[x], lambda d=d: beside(d), ("vx", d))
    for d in range(1, NX):
        arrive(parts.at[mod(x - d, NX)], ("vx", d))
    table[chip, core] = (parts[0] + parts[1]) + (parts[2] + parts[3])
    steps = [(dy, dz) for dz in range(NZ) for dy in range(NY) if (dy, dz) != (0, 0)]
    for dy, dz in steps:
        send(lambda: table.at[chip, core], lambda dy=dy, dz=dz: at(dy=dy, dz=dz), ("vp", dy, dz))
    for dy, dz in steps:
        arrive(table.at[mod(y - dy, NY) * NZ + mod(z - dz, NZ), core], ("vp", dy, dz))
    send(lambda: table.at[:, core], lambda: at(dc=1), ("vc",))
    arrive(table.at[:, lax.rem(core + 1, 2)], ("vc",))

    order = order_ref[...]
    rows = table[...].reshape(NROWS, HALF)
    lane = lax.broadcasted_iota(jnp.int32, (HALF, B), 0)
    pick = jnp.where(lane == order % HALF, 1.0, 0.0).astype(jnp.bfloat16)
    picked = jnp.zeros((NROWS, B), jnp.float32)
    for _ in range(3):
        piece = rows.astype(jnp.bfloat16)
        rows = rows - piece.astype(jnp.float32)
        picked = picked + jnp.dot(piece, pick, preferred_element_type=jnp.float32)
    line = lax.broadcasted_iota(jnp.int32, (NROWS, B), 0)
    variance_ref[...] = jnp.sum(jnp.where(line == order // HALF, picked, 0.0), axis=0, keepdims=True)
    for j in range(DESC):
        pltpu.make_async_copy(rounded.at[j], product_ref.at[j], local_sem.at[j]).wait()
    for op in pending:
        op().wait_send()

    @pl.when(core == 0)
    def _():
        finish_core0()

    @pl.when(core == 1)
    def _():
        finish_core1()

    assert len(sends) <= SEMS and len(recvs) <= SEMS


SEMS = 240
RING_ORDER = ("1", "2", "3", "0b", "0a")
HALF = B // 2
NROWS = NY * NZ * 2 * 2 * DESC


def body(sigma_tiles, panel_factor, panel_mask, inv_diagonal, subtree_of, partition_order):
    product, variance = pl.pallas_call(
        kernel,
        out_shape=(
            jax.ShapeDtypeStruct((DESC, CH, Q, B), jnp.bfloat16),
            jax.ShapeDtypeStruct((1, B), jnp.float32),
        ),
        in_specs=[pl.BlockSpec(memory_space=pltpu.HBM)] * 6,
        out_specs=(
            pl.BlockSpec(memory_space=pltpu.HBM),
            pl.BlockSpec(memory_space=pltpu.VMEM),
        ),
        scratch_shapes=[
            pltpu.VMEM((TILES, Q, B), jnp.bfloat16),
            pltpu.VMEM((CH * Q, CH * B), jnp.bfloat16),
            pltpu.VMEM((DESC, CH, B, B), jnp.bfloat16),
            pltpu.VMEM((DESC, CH, Q, B), jnp.bfloat16),
            pltpu.VMEM((DESC, CH, Q, B), jnp.bfloat16),
            pltpu.VMEM((NX, 2 * DESC, HALF), jnp.float32),
            pltpu.VMEM((NY * NZ, 2, 2 * DESC, HALF), jnp.float32),
            pltpu.SMEM((NY * NZ * 2,), jnp.int32),
            pltpu.SMEM((DESC, CH), jnp.int32),
            pltpu.VMEM((DESC, Q), jnp.float32),
            pltpu.VMEM((1, B), jnp.int32),
            pltpu.SemaphoreType.DMA((SEMS,)),
            pltpu.SemaphoreType.DMA((SEMS,)),
            pltpu.SemaphoreType.DMA((2 * DESC + 2,)),
            pltpu.SemaphoreType.DMA((4,)),
        ],
        compiler_params=pltpu.CompilerParams(
            collective_id=0, has_side_effects=True, vmem_limit_bytes=56 * 1024 * 1024
        ),
    )(subtree_of, panel_mask, inv_diagonal, partition_order.reshape(1, B), sigma_tiles, panel_factor)
    return -product, variance.reshape(B)


def solution(mesh):
    placed = (
        P("leaf", "panel", None),
        P("leaf", None, "panel", None),
        P("leaf", None),
        P("leaf", "panel"),
        P(),
        P(("leaf", "panel")),
    )
    return jax.shard_map(
        body,
        mesh=mesh,
        in_specs=placed,
        out_specs=(P("leaf", None, "panel", None), P(("leaf", "panel"))),
        check_vma=False,
    )
```

```python
import jax
import jax.numpy as jnp
from jax import lax
from jax.experimental import pallas as pl
from jax.experimental.pallas import tpu as pltpu
from jax.sharding import PartitionSpec as P

NX, NY, NZ = 4, 4, 8
CH = 15
B = 256
Q = 64
DESC = 4
NEAR = 12
FAR = (20, 8, 4, 3)
FAR_AT = (0, 20, 28, 32)
COLUMN = 35
FAR_BASE = NX * NY * NZ // NX * NEAR
TILES = FAR_BASE + NZ * COLUMN
Z_ORDER = (0, -1, 1, -2, 2, -3, 3, 4)
MESH = pl.DeviceIdType.MESH


def halves(count):
    return (0, (count + 1) // 2), ((count + 1) // 2, count // 2)


def kernel(
    subtree_hbm, mask_hbm, inv_hbm, order_hbm, sigma_ref, factor_ref,
    product_ref, variance_ref,
    tiles, lhs, full, own, rounded, parts, table, pick,
    subtree_ref, mask_ref, inv_ref, order_ref,
    send_sem, recv_sem, local_sem, small_sem,
):
    leaf = lax.axis_index("leaf")
    x = lax.axis_index("panel")
    core = lax.rem(leaf, 2)
    chip = leaf // 2
    y = chip // NZ
    z = lax.rem(chip, NZ)

    def mod(value, size):
        return lax.rem(value + 2 * size, size)

    def at(dy=0, dz=0, dc=0):
        return {"leaf": (mod(y + dy, NY) * NZ + mod(z + dz, NZ)) * 2 + lax.rem(core + dc, 2), "panel": x}

    def beside(dx):
        return {"leaf": leaf, "panel": mod(x + dx, NX)}

    sends = {}
    recvs = {}
    pending = []

    def number(names, name):
        if name not in names:
            names[name] = len(names)
        return names[name]

    def copy(src, dst, device, name):
        return pltpu.make_async_remote_copy(
            src_ref=src, dst_ref=dst,
            send_sem=send_sem.at[number(sends, name)],
            recv_sem=recv_sem.at[number(recvs, name)],
            device_id=device, device_id_type=MESH,
        )

    def send(ref, device, name, src=None):
        def build():
            return copy((src or ref)(), ref(), device(), name)

        build().start()
        pending.append(build)

    def arrive(ref, name):
        copy(ref, ref, beside(1), name).wait_recv()

    peers = [beside(1), beside(-1), at(dy=1), at(dy=-1), at(dz=1), at(dz=-1), at(dc=1)]
    barrier = pltpu.get_barrier_semaphore()
    for peer in peers:
        pl.semaphore_signal(barrier, inc=1, device_id=peer, device_id_type=MESH)

    def near(dy, dz, low=0, count=NEAR):
        row = mod(y + dy, NY) * NZ + mod(z + dz, NZ)
        return tiles.at[pl.ds(row * NEAR + low, count)]

    def far(dz, low=0, count=COLUMN):
        return tiles.at[pl.ds(FAR_BASE + mod(z + dz, NZ) * COLUMN + low, count)]

    def own_tiles(pieces):
        ops = [
            pltpu.make_async_copy(sigma_ref.at[pl.ds(src, ref.shape[0])], ref, local_sem.at[2 * DESC + k])
            for k, (src, ref) in enumerate(pieces)
        ]
        for op in ops:
            op.start()
        for op in ops:
            op.wait()

    for j in range(DESC):
        pltpu.make_async_copy(factor_ref.at[j], own.at[j], local_sem.at[j]).start()

    small = [
        pltpu.make_async_copy(src, dst, small_sem.at[k])
        for k, (src, dst) in enumerate((
            (mask_hbm, mask_ref), (subtree_hbm, subtree_ref), (inv_hbm, inv_ref), (order_hbm, order_ref),
        ))
    ]
    for op in small:
        op.start()

    @pl.when(core == 0)
    def _():
        group = jnp.where(y == 0, 0, z // 4)
        own_tiles([(0, near(0, 0, 0, 8)), (8 + 4 * group, near(0, 0, 8, 4))])

    for c in range(NY):
        @pl.when((core == 1) & (y == c))
        def _():
            if c == 0:
                own_tiles([(0, far(0, 4, 16))])
            elif c == 1:
                own_tiles([(4 * (z // 4), far(0, 20, 4)), (8 + 4 * (z // 4), far(0, 24, 4))])
            elif c == 2:
                own_tiles([(2 * (z // 2), far(0, 28, 2)), (8 + 2 * (z // 2), far(0, 30, 2))])
            else:
                own_tiles([(2 * (z // 2), far(0, 32, 2)), (8 + z, far(0, 34, 1))])

    for op in small:
        op.wait()
    for j in range(DESC):
        pltpu.make_async_copy(factor_ref.at[j], own.at[j], local_sem.at[j]).wait()
        for b in range(CH):
            own[j, b] = own[j, b] * mask_ref[j, b].astype(jnp.bfloat16)
    pl.semaphore_wait(barrier, len(peers))

    def quarter(j, dx, low=0, count=CH):
        return full.at[j, pl.ds(low, count), pl.ds(pl.multiple_of(mod(x + dx, NX) * Q, Q), Q)]

    def factor_parts(j):
        first = 8 - j % 2
        return (0, first), (first, CH - first)

    def factor_start(j):
        send(lambda: quarter(j, 0), lambda: beside(1), ("fr", j), src=lambda: own.at[j])
        send(lambda: quarter(j, 0), lambda: beside(-1), ("fl", j), src=lambda: own.at[j])
        pltpu.make_async_copy(own.at[j], quarter(j, 0), local_sem.at[DESC + j]).start()

    def factor_forward(j):
        right, left = factor_parts(j)
        arrive(quarter(j, -1), ("fr", j))
        send(lambda: quarter(j, -1, *right), lambda: beside(1), ("fr2", j))
        arrive(quarter(j, 1), ("fl", j))
        send(lambda: quarter(j, 1, *left), lambda: beside(-1), ("fl2", j))

    def factor_done(j):
        right, left = factor_parts(j)
        arrive(quarter(j, 2, *right), ("fr2", j))
        arrive(quarter(j, 2, *left), ("fl2", j))
        pltpu.make_async_copy(own.at[j], quarter(j, 0), local_sem.at[DESC + j]).wait()

    first6, last6 = halves(NEAR)
    near_chunks = [(dy, dz) for dy in range(NY) for dz in Z_ORDER]

    def run_core0():
        def to_peer(dy, dz):
            send(lambda: near(dy, dz), lambda: at(dc=1), ("n", dy % NY, dz))

        def along_y(dz):
            send(lambda: near(0, dz), lambda: at(dy=1), ("yu", dz))
            send(lambda: near(0, dz), lambda: at(dy=-1), ("yd", dz))
            to_peer(0, dz)

        def start():
            @pl.when(y == 0)
            def _():
                ref = far(0, 0, 4)
                copy(sigma_ref.at[pl.ds(12, 4)], ref, at(dc=1), ("extra",)).start()

            send(lambda: near(0, 0), lambda: at(dz=1), ("zr", 1))
            send(lambda: near(0, 0), lambda: at(dz=-1), ("zl", 1))
            along_y(0)

        def ring(d):
            arrive(near(0, -d), ("zr", d))
            if d < 3:
                send(lambda: near(0, -d), lambda: at(dz=1), ("zr", d + 1))
            else:
                send(lambda: near(0, -d, *first6), lambda: at(dz=1), ("zr", 4))
            arrive(near(0, d), ("zl", d))
            if d < 3:
                send(lambda: near(0, d), lambda: at(dz=-1), ("zl", d + 1))
            else:
                send(lambda: near(0, d, *last6), lambda: at(dz=-1), ("zl", 4))
            along_y(-d)
            along_y(d)

        def ring_end():
            arrive(near(0, 4, *first6), ("zr", 4))
            arrive(near(0, 4, *last6), ("zl", 4))
            along_y(4)

        def cross(dz):
            arrive(near(-1, dz), ("yu", dz))
            send(lambda: near(-1, dz, *first6), lambda: at(dy=1), ("yu2", dz))
            arrive(near(1, dz), ("yd", dz))
            send(lambda: near(1, dz, *last6), lambda: at(dy=-1), ("yd2", dz))
            to_peer(-1, dz)
            to_peer(1, dz)

        def cross_end(dz):
            arrive(near(2, dz, *first6), ("yu2", dz))
            arrive(near(2, dz, *last6), ("yd2", dz))
            to_peer(2, dz)

        events = [(0, 0, lambda: factor_start(0)), (0, 1, start)]
        events += [(0, 2 + j, lambda j=j: factor_start(j)) for j in range(1, DESC)]
        events += [(5 * d, 1, lambda d=d: ring(d)) for d in range(1, 4)]
        events += [(17, 1, ring_end)]
        for k, dz in enumerate(Z_ORDER):
            events += [(6 * (k + 1), 2, lambda dz=dz: cross(dz)), (6 * (k + 2), 3, lambda dz=dz: cross_end(dz))]
        events += [(10 * j + 8, 4, lambda j=j: factor_forward(j)) for j in range(DESC)]
        for _, _, event in sorted(events, key=lambda e: e[:2]):
            event()
        for dz in Z_ORDER:
            for which in range(2):
                low, count = halves(FAR[0])[which]
                arrive(far(dz, low, count), ("p", "0" + "ab"[which], dz))
            for c in range(1, NY):
                arrive(far(dz, FAR_AT[c], FAR[c]), ("p", str(c), dz))

    def finish_core0():
        for op in sent[0]:
            op().wait_send()

        @pl.when(y == 0)
        def _():
            copy(sigma_ref.at[pl.ds(12, 4)], far(0, 0, 4), at(dc=1), ("extra",)).wait_send()

    later = []

    def run_core1():
        def part(c, which):
            low, count = halves(FAR[c])[which]
            return (FAR_AT[c] + low, count)

        def only(row, action):
            before = len(pending)

            @pl.when(y == row)
            def _():
                action()

            for op in pending[before:]:
                later.append((row, op))
            del pending[before:]

        def around(c, which):
            low, count = part(c, which) if c == 0 else (FAR_AT[c], FAR[c])
            name = piece_name(c, which)
            send(lambda: far(0, low, count), lambda: at(dz=1), ("zr" + name, 1))
            send(lambda: far(0, low, count), lambda: at(dz=-1), ("zl" + name, 1))
            send(lambda: far(0, low, count), lambda: at(dc=1), ("p", name, 0))

        def piece_name(c, which):
            return "0" + "ab"[which] if c == 0 else str(c)

        def across_send(c, which, up):
            send(lambda: far(0, *part(c, which)), lambda: at(dy=1 if up else -1), ("c", up, which))

        def load_own(c):
            across_send(c, 1, False)
            if c == 0:
                around(0, 1)
                arrive(far(0, 0, 4), ("extra",))
            across_send(c, 0, True)
            across_send(c, 0, False)
            across_send(c, 1, True)
            around(c, 0)

        def from_below(c):
            arrive(far(0, *part(c, 0)), ("c", True, 0))
            send(lambda: far(0, *part(c, 0)), lambda: at(dy=1), ("c2", 0))

        def from_above(c):
            arrive(far(0, *part(c, 1)), ("c", False, 1))
            send(lambda: far(0, *part(c, 1)), lambda: at(dy=-1), ("c2", 1))

        def rest_below(c):
            if c == 0:
                around(0, 0)
            arrive(far(0, *part(c, 1)), ("c", True, 1))
            around(c, 1)

        def rest_above(c):
            if c == 0:
                around(0, 1)
            arrive(far(0, *part(c, 0)), ("c", False, 0))
            around(c, 0)

        def from_two(c):
            arrive(far(0, *part(c, 1)), ("c2", 1))
            if c == 0:
                around(0, 1)
            arrive(far(0, *part(c, 0)), ("c2", 0))
            around(c, 0)

        def start():
            for c in range(NY):
                only(c, lambda c=c: load_own(c))

        def across():
            for action, dy in ((from_below, 1), (from_above, -1), (rest_below, 1), (rest_above, -1)):
                for c in range(NY):
                    only((c + dy) % NY, lambda c=c, action=action: action(c))

        def across_end():
            for c in range(NY):
                only((c + 2) % NY, lambda c=c: from_two(c))

        rings = {
            "0a": (part(0, 0), part(0, 0), None),
            "0b": (part(0, 1), None, part(0, 1)),
        }
        for c in range(1, NY):
            rings[str(c)] = ((FAR_AT[c], FAR[c]), part(c, 0), part(c, 1))

        def ring(name, d):
            whole, right, left = rings[name]
            arrive(far(-d, *whole), ("zr" + name, d))
            right = whole if d < 3 else right
            if right:
                send(lambda: far(-d, *right), lambda: at(dz=1), ("zr" + name, d + 1))
            arrive(far(d, *whole), ("zl" + name, d))
            left = whole if d < 3 else left
            if left:
                send(lambda: far(d, *left), lambda: at(dz=-1), ("zl" + name, d + 1))
            send(lambda: far(-d, *whole), lambda: at(dc=1), ("p", name, -d))
            send(lambda: far(d, *whole), lambda: at(dc=1), ("p", name, d))

        def ring_end(name):
            whole, right, left = rings[name]
            if right:
                arrive(far(4, *right), ("zr" + name, 4))
            if left:
                arrive(far(4, *left), ("zl" + name, 4))
            send(lambda: far(4, *whole), lambda: at(dc=1), ("p", name, 4))

        events = [(0, 0, lambda: factor_start(0)), (0, 1, start)]
        events += [(0, 2 + j, lambda j=j: factor_start(j)) for j in range(1, DESC)]
        events += [(5, 1, across), (8, 1, across_end)]
        for k, name in enumerate(RING_ORDER):
            events += [(11 + 12 * d + 2 * k, 1, lambda d=d, name=name: ring(name, d)) for d in range(1, 4)]
            events += [(59 + k, 1, lambda name=name: ring_end(name))]
        events += [(10 * j + 8, 4, lambda j=j: factor_forward(j)) for j in range(DESC)]
        for _, _, event in sorted(events, key=lambda e: e[:2]):
            event()
        for dy, dz in near_chunks:
            arrive(near(dy, dz), ("n", dy, dz))

    def finish_core1():
        for op in sent[1]:
            op().wait_send()
        for row, op in later:
            @pl.when(y == row)
            def _():
                op().wait_send()

    @pl.when(core == 0)
    def _():
        run_core0()

    sent = [list(pending)]
    pending.clear()

    @pl.when(core == 1)
    def _():
        run_core1()

    sent.append(list(pending))
    pending.clear()

    subtree = subtree_ref[leaf]
    upper, middle, lower = subtree // 8, subtree // 4, subtree // 2

    def place(a, row, slots):
        for b, slot in enumerate(slots):
            lhs[pl.ds(pl.multiple_of(a * Q, Q), Q), pl.ds(b * B, B)] = tiles[slot]

    def near_slots(row, count):
        return [row * NEAR + k for k in range(count)]

    def column(row):
        return FAR_BASE + lax.rem(row, NZ) * COLUMN

    @pl.loop(0, 8)
    def _(a):
        base = column(a)
        mine = jnp.where(upper == 0, a * NEAR + 8, base)
        slots = near_slots(a, 8) + [mine + k for k in range(4)]
        place(a, a, slots + [base + 4 + 2 * middle, base + 5 + 2 * middle, base + 12 + lower])

    @pl.loop(0, 4)
    def _(i):
        row = 8 + 4 * upper + i
        base = column(row) + FAR_AT[1]
        pair = base + 2 * (middle - 2 * upper)
        place(8 + i, row, near_slots(row, NEAR) + [pair, pair + 1, base + 4 + lower - 4 * upper])

    @pl.loop(0, 2)
    def _(i):
        row = 16 + 2 * middle + i
        base = column(row) + FAR_AT[2]
        place(12 + i, row, near_slots(row, NEAR) + [base, base + 1, base + 2 + lower - 2 * middle])

    row = 24 + lower
    base = column(row) + FAR_AT[3]
    place(14, row, near_slots(row, NEAR) + [base, base + 1, base + 2])

    spot = lax.broadcasted_iota(jnp.int32, (1, HALF), 1) // Q

    @pl.loop(0, DESC)
    def _(j):
        for k in range(DESC):
            @pl.when(j == k)
            def _():
                factor_done(k)

        product = jnp.dot(lhs[...], full[j].reshape(CH * B, B), preferred_element_type=jnp.float32)
        product = product.reshape(CH, Q, B)
        rounded[j] = product.astype(jnp.bfloat16)
        pltpu.make_async_copy(rounded.at[j], product_ref.at[j], local_sem.at[j]).start()
        total = jnp.sum(own[j].astype(jnp.float32) * product, axis=(0, 1), keepdims=True)[0]
        inverse = inv_ref[pl.ds(j, 1)]
        inverse = jnp.concatenate([inverse, inverse], axis=1)
        for half in range(2):
            share = jnp.where(spot + 2 * half == x, inverse, 0.0)
            parts[x, pl.ds(2 * j + half, 1)] = total[:, half * HALF:(half + 1) * HALF] + share

    for d in range(1, NX):
        send(lambda: parts.at[x], lambda d=d: beside(d), ("vx", d))
    order = order_ref[...]
    lane = lax.broadcasted_iota(jnp.int32, (HALF, B), 0)
    pick[...] = jnp.where(lane == order % HALF, 1.0, 0.0).astype(jnp.bfloat16)

    @pl.when(core == 0)
    def _():
        finish_core0()

    @pl.when(core == 1)
    def _():
        finish_core1()

    for d in range(1, NX):
        arrive(parts.at[mod(x - d, NX)], ("vx", d))
    table[chip, core] = (parts[0] + parts[1]) + (parts[2] + parts[3])
    steps = [(dy, dz) for dz in range(NZ) for dy in range(NY) if (dy, dz) != (0, 0)]
    for dy, dz in steps:
        send(lambda: table.at[chip, core], lambda dy=dy, dz=dz: at(dy=dy, dz=dz), ("vp", dy, dz))
    for dy, dz in steps:
        arrive(table.at[mod(y - dy, NY) * NZ + mod(z - dz, NZ), core], ("vp", dy, dz))
    send(lambda: table.at[:, core], lambda: at(dc=1), ("vc",))
    arrive(table.at[:, lax.rem(core + 1, 2)], ("vc",))

    rows = table[...].reshape(NROWS, HALF)
    picked = jnp.zeros((NROWS, B), jnp.float32)
    for _ in range(3):
        piece = rows.astype(jnp.bfloat16)
        rows = rows - piece.astype(jnp.float32)
        picked = picked + jnp.dot(piece, pick[...], preferred_element_type=jnp.float32)
    line = lax.broadcasted_iota(jnp.int32, (NROWS, B), 0)
    variance_ref[...] = jnp.sum(jnp.where(line == order // HALF, picked, 0.0), axis=0, keepdims=True)
    for j in range(DESC):
        pltpu.make_async_copy(rounded.at[j], product_ref.at[j], local_sem.at[j]).wait()
    for op in pending:
        op().wait_send()

    assert len(sends) <= SEMS and len(recvs) <= SEMS


SEMS = 240
RING_ORDER = ("0b", "0a", "1", "2", "3")
HALF = B // 2
NROWS = NY * NZ * 2 * 2 * DESC


def body(sigma_tiles, panel_factor, panel_mask, inv_diagonal, subtree_of, partition_order):
    product, variance = pl.pallas_call(
        kernel,
        out_shape=(
            jax.ShapeDtypeStruct((DESC, CH, Q, B), jnp.bfloat16),
            jax.ShapeDtypeStruct((1, B), jnp.float32),
        ),
        in_specs=[pl.BlockSpec(memory_space=pltpu.HBM)] * 6,
        out_specs=(
            pl.BlockSpec(memory_space=pltpu.HBM),
            pl.BlockSpec(memory_space=pltpu.VMEM),
        ),
        scratch_shapes=[
            pltpu.VMEM((TILES, Q, B), jnp.bfloat16),
            pltpu.VMEM((CH * Q, CH * B), jnp.bfloat16),
            pltpu.VMEM((DESC, CH, B, B), jnp.bfloat16),
            pltpu.VMEM((DESC, CH, Q, B), jnp.bfloat16),
            pltpu.VMEM((DESC, CH, Q, B), jnp.bfloat16),
            pltpu.VMEM((NX, 2 * DESC, HALF), jnp.float32),
            pltpu.VMEM((NY * NZ, 2, 2 * DESC, HALF), jnp.float32),
            pltpu.VMEM((HALF, B), jnp.bfloat16),
            pltpu.SMEM((NY * NZ * 2,), jnp.int32),
            pltpu.SMEM((DESC, CH), jnp.int32),
            pltpu.VMEM((DESC, Q), jnp.float32),
            pltpu.VMEM((1, B), jnp.int32),
            pltpu.SemaphoreType.DMA((SEMS,)),
            pltpu.SemaphoreType.DMA((SEMS,)),
            pltpu.SemaphoreType.DMA((2 * DESC + 2,)),
            pltpu.SemaphoreType.DMA((4,)),
        ],
        compiler_params=pltpu.CompilerParams(
            collective_id=0, has_side_effects=True, vmem_limit_bytes=56 * 1024 * 1024
        ),
    )(subtree_of, panel_mask, inv_diagonal, partition_order.reshape(1, B), sigma_tiles, panel_factor)
    return -product, variance.reshape(B)


def solution(mesh):
    placed = (
        P("leaf", "panel", None),
        P("leaf", None, "panel", None),
        P("leaf", None),
        P("leaf", "panel"),
        P(),
        P(("leaf", "panel")),
    )
    return jax.shard_map(
        body,
        mesh=mesh,
        in_specs=placed,
        out_specs=(P("leaf", None, "panel", None), P(("leaf", "panel"))),
        check_vma=False,
    )
```

```python
import jax
import jax.numpy as jnp
from jax import lax
from jax.experimental import pallas as pl
from jax.experimental.pallas import tpu as pltpu
from jax.sharding import PartitionSpec as P

NX, NY, NZ = 4, 4, 8
CH = 15
B = 256
Q = 64
DESC = 4
NEAR = 12
FAR = (20, 8, 4, 3)
FAR_AT = (0, 20, 28, 32)
COLUMN = 35
FAR_BASE = NX * NY * NZ // NX * NEAR
TILES = FAR_BASE + NZ * COLUMN
Z_ORDER = (0, -1, 1, -2, 2, -3, 3, 4)
MESH = pl.DeviceIdType.MESH


def halves(count):
    return (0, (count + 1) // 2), ((count + 1) // 2, count // 2)


def kernel(
    subtree_hbm, mask_hbm, inv_hbm, order_hbm, sigma_ref, factor_ref,
    product_ref, variance_ref,
    tiles, lhs, full, own, rounded, parts, table, pick,
    subtree_ref, mask_ref, inv_ref, order_ref,
    send_sem, recv_sem, local_sem, small_sem,
):
    leaf = lax.axis_index("leaf")
    x = lax.axis_index("panel")
    core = lax.rem(leaf, 2)
    chip = leaf // 2
    y = chip // NZ
    z = lax.rem(chip, NZ)

    def mod(value, size):
        return lax.rem(value + 2 * size, size)

    def at(dy=0, dz=0, dc=0):
        return {"leaf": (mod(y + dy, NY) * NZ + mod(z + dz, NZ)) * 2 + lax.rem(core + dc, 2), "panel": x}

    def beside(dx):
        return {"leaf": leaf, "panel": mod(x + dx, NX)}

    sends = {}
    recvs = {}
    pending = []

    def number(names, name):
        if name not in names:
            names[name] = len(names)
        return names[name]

    def copy(src, dst, device, name):
        return pltpu.make_async_remote_copy(
            src_ref=src, dst_ref=dst,
            send_sem=send_sem.at[number(sends, name)],
            recv_sem=recv_sem.at[number(recvs, name)],
            device_id=device, device_id_type=MESH,
        )

    def send(ref, device, name, src=None):
        def build():
            return copy((src or ref)(), ref(), device(), name)

        build().start()
        pending.append(build)

    def arrive(ref, name):
        copy(ref, ref, beside(1), name).wait_recv()

    peers = [beside(1), beside(-1), at(dy=1), at(dy=-1), at(dz=1), at(dz=-1), at(dc=1)]
    barrier = pltpu.get_barrier_semaphore()
    for peer in peers:
        pl.semaphore_signal(barrier, inc=1, device_id=peer, device_id_type=MESH)

    def near(dy, dz, low=0, count=NEAR):
        row = mod(y + dy, NY) * NZ + mod(z + dz, NZ)
        return tiles.at[pl.ds(row * NEAR + low, count)]

    def far(dz, low=0, count=COLUMN):
        return tiles.at[pl.ds(FAR_BASE + mod(z + dz, NZ) * COLUMN + low, count)]

    def own_tiles(pieces):
        ops = [
            pltpu.make_async_copy(sigma_ref.at[pl.ds(src, ref.shape[0])], ref, local_sem.at[2 * DESC + k])
            for k, (src, ref) in enumerate(pieces)
        ]
        for op in ops:
            op.start()
        for op in ops:
            op.wait()

    for j in range(DESC):
        pltpu.make_async_copy(factor_ref.at[j], own.at[j], local_sem.at[j]).start()

    small = [
        pltpu.make_async_copy(src, dst, small_sem.at[k])
        for k, (src, dst) in enumerate((
            (mask_hbm, mask_ref), (subtree_hbm, subtree_ref), (inv_hbm, inv_ref), (order_hbm, order_ref),
        ))
    ]
    for op in small:
        op.start()

    @pl.when(core == 0)
    def _():
        group = jnp.where(y == 0, 0, z // 4)
        own_tiles([(0, near(0, 0, 0, 8)), (8 + 4 * group, near(0, 0, 8, 4))])

    for c in range(NY):
        @pl.when((core == 1) & (y == c))
        def _():
            if c == 0:
                own_tiles([(0, far(0, 4, 16))])
            elif c == 1:
                own_tiles([(4 * (z // 4), far(0, 20, 4)), (8 + 4 * (z // 4), far(0, 24, 4))])
            elif c == 2:
                own_tiles([(2 * (z // 2), far(0, 28, 2)), (8 + 2 * (z // 2), far(0, 30, 2))])
            else:
                own_tiles([(2 * (z // 2), far(0, 32, 2)), (8 + z, far(0, 34, 1))])

    for op in small:
        op.wait()
    for j in range(DESC):
        pltpu.make_async_copy(factor_ref.at[j], own.at[j], local_sem.at[j]).wait()
        for b in range(CH):
            own[j, b] = own[j, b] * mask_ref[j, b].astype(jnp.bfloat16)
    pl.semaphore_wait(barrier, len(peers))

    def quarter(j, dx, low=0, count=CH):
        return full.at[j, pl.ds(low, count), pl.ds(pl.multiple_of(mod(x + dx, NX) * Q, Q), Q)]

    def factor_parts(j):
        first = 8 - j % 2
        return (0, first), (first, CH - first)

    def factor_start(j):
        send(lambda: quarter(j, 0), lambda: beside(1), ("fr", j), src=lambda: own.at[j])
        send(lambda: quarter(j, 0), lambda: beside(-1), ("fl", j), src=lambda: own.at[j])
        pltpu.make_async_copy(own.at[j], quarter(j, 0), local_sem.at[DESC + j]).start()

    def factor_forward(j):
        right, left = factor_parts(j)
        arrive(quarter(j, -1), ("fr", j))
        send(lambda: quarter(j, -1, *right), lambda: beside(1), ("fr2", j))
        arrive(quarter(j, 1), ("fl", j))
        send(lambda: quarter(j, 1, *left), lambda: beside(-1), ("fl2", j))

    def factor_done(j):
        right, left = factor_parts(j)
        arrive(quarter(j, 2, *right), ("fr2", j))
        arrive(quarter(j, 2, *left), ("fl2", j))
        pltpu.make_async_copy(own.at[j], quarter(j, 0), local_sem.at[DESC + j]).wait()

    first6, last6 = halves(NEAR)
    near_chunks = [(dy, dz) for dy in range(NY) for dz in Z_ORDER]

    def run_core0():
        def to_peer(dy, dz):
            send(lambda: near(dy, dz), lambda: at(dc=1), ("n", dy % NY, dz))

        def along_y(dz):
            send(lambda: near(0, dz), lambda: at(dy=1), ("yu", dz))
            send(lambda: near(0, dz), lambda: at(dy=-1), ("yd", dz))
            to_peer(0, dz)

        def start():
            @pl.when(y == 0)
            def _():
                ref = far(0, 0, 4)
                copy(sigma_ref.at[pl.ds(12, 4)], ref, at(dc=1), ("extra",)).start()

            send(lambda: near(0, 0), lambda: at(dz=1), ("zr", 1))
            send(lambda: near(0, 0), lambda: at(dz=-1), ("zl", 1))
            along_y(0)

        def ring(d):
            arrive(near(0, -d), ("zr", d))
            if d < 3:
                send(lambda: near(0, -d), lambda: at(dz=1), ("zr", d + 1))
            else:
                send(lambda: near(0, -d, *first6), lambda: at(dz=1), ("zr", 4))
            arrive(near(0, d), ("zl", d))
            if d < 3:
                send(lambda: near(0, d), lambda: at(dz=-1), ("zl", d + 1))
            else:
                send(lambda: near(0, d, *last6), lambda: at(dz=-1), ("zl", 4))
            along_y(-d)
            along_y(d)

        def ring_end():
            arrive(near(0, 4, *first6), ("zr", 4))
            arrive(near(0, 4, *last6), ("zl", 4))
            along_y(4)

        def cross(dz):
            arrive(near(-1, dz), ("yu", dz))
            send(lambda: near(-1, dz, *first6), lambda: at(dy=1), ("yu2", dz))
            arrive(near(1, dz), ("yd", dz))
            send(lambda: near(1, dz, *last6), lambda: at(dy=-1), ("yd2", dz))
            to_peer(-1, dz)
            to_peer(1, dz)

        def cross_end(dz):
            arrive(near(2, dz, *first6), ("yu2", dz))
            arrive(near(2, dz, *last6), ("yd2", dz))
            to_peer(2, dz)

        events = [(0, 0, lambda: factor_start(0)), (0, 1, start)]
        events += [(0, 2 + j, lambda j=j: factor_start(j)) for j in range(1, DESC)]
        events += [(5 * d, 1, lambda d=d: ring(d)) for d in range(1, 4)]
        events += [(17, 1, ring_end)]
        for k, dz in enumerate(Z_ORDER):
            events += [(5 * (k + 1) + 8, 2, lambda dz=dz: cross(dz)), (5 * (k + 1) + 20, 3, lambda dz=dz: cross_end(dz))]
        events += [(10 * j + 8, 4, lambda j=j: factor_forward(j)) for j in range(DESC)]
        for _, _, event in sorted(events, key=lambda e: e[:2]):
            event()
        for dz in Z_ORDER:
            for which in range(2):
                low, count = halves(FAR[0])[which]
                arrive(far(dz, low, count), ("p", "0" + "ab"[which], dz))
            for c in range(1, NY):
                arrive(far(dz, FAR_AT[c], FAR[c]), ("p", str(c), dz))

    def finish_core0():
        for op in sent[0]:
            op().wait_send()

        @pl.when(y == 0)
        def _():
            copy(sigma_ref.at[pl.ds(12, 4)], far(0, 0, 4), at(dc=1), ("extra",)).wait_send()

    later = []

    def run_core1():
        def part(c, which):
            low, count = halves(FAR[c])[which]
            return (FAR_AT[c] + low, count)

        def only(row, action):
            before = len(pending)

            @pl.when(y == row)
            def _():
                action()

            for op in pending[before:]:
                later.append((row, op))
            del pending[before:]

        def around(c, which):
            low, count = part(c, which) if c == 0 else (FAR_AT[c], FAR[c])
            name = piece_name(c, which)
            send(lambda: far(0, low, count), lambda: at(dz=1), ("zr" + name, 1))
            send(lambda: far(0, low, count), lambda: at(dz=-1), ("zl" + name, 1))
            send(lambda: far(0, low, count), lambda: at(dc=1), ("p", name, 0))

        def piece_name(c, which):
            return "0" + "ab"[which] if c == 0 else str(c)

        def across_send(c, which, up):
            send(lambda: far(0, *part(c, which)), lambda: at(dy=1 if up else -1), ("c", up, which))

        def load_own(c):
            across_send(c, 1, False)
            if c == 0:
                around(0, 1)
                arrive(far(0, 0, 4), ("extra",))
            across_send(c, 0, True)
            across_send(c, 0, False)
            across_send(c, 1, True)
            around(c, 0)

        def from_below(c):
            arrive(far(0, *part(c, 0)), ("c", True, 0))
            send(lambda: far(0, *part(c, 0)), lambda: at(dy=1), ("c2", 0))

        def from_above(c):
            arrive(far(0, *part(c, 1)), ("c", False, 1))
            send(lambda: far(0, *part(c, 1)), lambda: at(dy=-1), ("c2", 1))

        def rest_below(c):
            if c == 0:
                around(0, 0)
            arrive(far(0, *part(c, 1)), ("c", True, 1))
            around(c, 1)

        def rest_above(c):
            if c == 0:
                around(0, 1)
            arrive(far(0, *part(c, 0)), ("c", False, 0))
            around(c, 0)

        def from_two(c):
            arrive(far(0, *part(c, 1)), ("c2", 1))
            if c == 0:
                around(0, 1)
            arrive(far(0, *part(c, 0)), ("c2", 0))
            around(c, 0)

        def start():
            for c in range(NY):
                only(c, lambda c=c: load_own(c))

        def across():
            for action, dy in ((from_below, 1), (from_above, -1), (rest_below, 1), (rest_above, -1)):
                for c in range(NY):
                    only((c + dy) % NY, lambda c=c, action=action: action(c))

        def across_end():
            for c in range(NY):
                only((c + 2) % NY, lambda c=c: from_two(c))

        rings = {
            "0a": (part(0, 0), part(0, 0), None),
            "0b": (part(0, 1), None, part(0, 1)),
        }
        for c in range(1, NY):
            rings[str(c)] = ((FAR_AT[c], FAR[c]), part(c, 0), part(c, 1))

        def ring(name, d):
            whole, right, left = rings[name]
            arrive(far(-d, *whole), ("zr" + name, d))
            right = whole if d < 3 else right
            if right:
                send(lambda: far(-d, *right), lambda: at(dz=1), ("zr" + name, d + 1))
            arrive(far(d, *whole), ("zl" + name, d))
            left = whole if d < 3 else left
            if left:
                send(lambda: far(d, *left), lambda: at(dz=-1), ("zl" + name, d + 1))
            send(lambda: far(-d, *whole), lambda: at(dc=1), ("p", name, -d))
            send(lambda: far(d, *whole), lambda: at(dc=1), ("p", name, d))

        def ring_end(name):
            whole, right, left = rings[name]
            if right:
                arrive(far(4, *right), ("zr" + name, 4))
            if left:
                arrive(far(4, *left), ("zl" + name, 4))
            send(lambda: far(4, *whole), lambda: at(dc=1), ("p", name, 4))

        events = [(0, 0, lambda: factor_start(0)), (0, 1, start)]
        events += [(0, 2 + j, lambda j=j: factor_start(j)) for j in range(1, DESC)]
        events += [(5, 1, across), (8, 1, across_end)]
        for k, name in enumerate(RING_ORDER):
            events += [(11 + 12 * d + 2 * k, 1, lambda d=d, name=name: ring(name, d)) for d in range(1, 4)]
            events += [(59 + k, 1, lambda name=name: ring_end(name))]
        events += [(10 * j + 8, 4, lambda j=j: factor_forward(j)) for j in range(DESC)]
        for _, _, event in sorted(events, key=lambda e: e[:2]):
            event()
        for dy, dz in near_chunks:
            arrive(near(dy, dz), ("n", dy, dz))

    def finish_core1():
        for op in sent[1]:
            op().wait_send()
        for row, op in later:
            @pl.when(y == row)
            def _():
                op().wait_send()

    @pl.when(core == 0)
    def _():
        run_core0()

    sent = [list(pending)]
    pending.clear()

    @pl.when(core == 1)
    def _():
        run_core1()

    sent.append(list(pending))
    pending.clear()

    subtree = subtree_ref[leaf]
    upper, middle, lower = subtree // 8, subtree // 4, subtree // 2

    def place(a, row, slots):
        for b, slot in enumerate(slots):
            lhs[pl.ds(pl.multiple_of(a * Q, Q), Q), pl.ds(b * B, B)] = tiles[slot]

    def near_slots(row, count):
        return [row * NEAR + k for k in range(count)]

    def column(row):
        return FAR_BASE + lax.rem(row, NZ) * COLUMN

    @pl.loop(0, 8)
    def _(a):
        base = column(a)
        mine = jnp.where(upper == 0, a * NEAR + 8, base)
        slots = near_slots(a, 8) + [mine + k for k in range(4)]
        place(a, a, slots + [base + 4 + 2 * middle, base + 5 + 2 * middle, base + 12 + lower])

    @pl.loop(0, 4)
    def _(i):
        row = 8 + 4 * upper + i
        base = column(row) + FAR_AT[1]
        pair = base + 2 * (middle - 2 * upper)
        place(8 + i, row, near_slots(row, NEAR) + [pair, pair + 1, base + 4 + lower - 4 * upper])

    @pl.loop(0, 2)
    def _(i):
        row = 16 + 2 * middle + i
        base = column(row) + FAR_AT[2]
        place(12 + i, row, near_slots(row, NEAR) + [base, base + 1, base + 2 + lower - 2 * middle])

    row = 24 + lower
    base = column(row) + FAR_AT[3]
    place(14, row, near_slots(row, NEAR) + [base, base + 1, base + 2])

    spot = lax.broadcasted_iota(jnp.int32, (1, HALF), 1) // Q

    @pl.loop(0, DESC)
    def _(j):
        for k in range(DESC):
            @pl.when(j == k)
            def _():
                factor_done(k)

        product = jnp.dot(lhs[...], full[j].reshape(CH * B, B), preferred_element_type=jnp.float32)
        product = product.reshape(CH, Q, B)
        rounded[j] = product.astype(jnp.bfloat16)
        pltpu.make_async_copy(rounded.at[j], product_ref.at[j], local_sem.at[j]).start()
        total = jnp.sum(own[j].astype(jnp.float32) * product, axis=(0, 1), keepdims=True)[0]
        inverse = inv_ref[pl.ds(j, 1)]
        inverse = jnp.concatenate([inverse, inverse], axis=1)
        for half in range(2):
            share = jnp.where(spot + 2 * half == x, inverse, 0.0)
            parts[x, pl.ds(2 * j + half, 1)] = total[:, half * HALF:(half + 1) * HALF] + share

    for d in range(1, NX):
        send(lambda: parts.at[x], lambda d=d: beside(d), ("vx", d))
    order = order_ref[...]
    lane = lax.broadcasted_iota(jnp.int32, (HALF, B), 0)
    pick[...] = jnp.where(lane == order % HALF, 1.0, 0.0).astype(jnp.bfloat16)

    @pl.when(core == 0)
    def _():
        finish_core0()

    @pl.when(core == 1)
    def _():
        finish_core1()

    for d in range(1, NX):
        arrive(parts.at[mod(x - d, NX)], ("vx", d))
    table[chip, core] = (parts[0] + parts[1]) + (parts[2] + parts[3])
    steps = [(dy, dz) for dz in range(NZ) for dy in range(NY) if (dy, dz) != (0, 0)]
    for dy, dz in steps:
        send(lambda: table.at[chip, core], lambda dy=dy, dz=dz: at(dy=dy, dz=dz), ("vp", dy, dz))

    def block(dy, dz, side):
        return table.at[mod(y - dy, NY) * NZ + mod(z - dz, NZ), lax.rem(core + side, 2)]

    steps.sort(key=lambda step: min(step[0], NY - step[0]) + min(step[1], NZ - step[1]))
    for dy, dz in [(0, 0)] + steps:
        if (dy, dz) != (0, 0):
            arrive(block(dy, dz, 0), ("vp", dy, dz))
        send(lambda dy=dy, dz=dz: block(dy, dz, 0), lambda: at(dc=1), ("vc", dy, dz))
    for dy, dz in [(0, 0)] + steps:
        arrive(block(dy, dz, 1), ("vc", dy, dz))

    rows = table[...].reshape(NROWS, HALF)
    picked = jnp.zeros((NROWS, B), jnp.float32)
    for _ in range(3):
        piece = rows.astype(jnp.bfloat16)
        rows = rows - piece.astype(jnp.float32)
        picked = picked + jnp.dot(piece, pick[...], preferred_element_type=jnp.float32)
    line = lax.broadcasted_iota(jnp.int32, (NROWS, B), 0)
    variance_ref[...] = jnp.sum(jnp.where(line == order // HALF, picked, 0.0), axis=0, keepdims=True)
    for j in range(DESC):
        pltpu.make_async_copy(rounded.at[j], product_ref.at[j], local_sem.at[j]).wait()
    for op in pending:
        op().wait_send()

    assert len(sends) <= SEMS and len(recvs) <= SEMS


SEMS = 240
RING_ORDER = ("0b", "0a", "1", "2", "3")
HALF = B // 2
NROWS = NY * NZ * 2 * 2 * DESC


def body(sigma_tiles, panel_factor, panel_mask, inv_diagonal, subtree_of, partition_order):
    product, variance = pl.pallas_call(
        kernel,
        out_shape=(
            jax.ShapeDtypeStruct((DESC, CH, Q, B), jnp.bfloat16),
            jax.ShapeDtypeStruct((1, B), jnp.float32),
        ),
        in_specs=[pl.BlockSpec(memory_space=pltpu.HBM)] * 6,
        out_specs=(
            pl.BlockSpec(memory_space=pltpu.HBM),
            pl.BlockSpec(memory_space=pltpu.VMEM),
        ),
        scratch_shapes=[
            pltpu.VMEM((TILES, Q, B), jnp.bfloat16),
            pltpu.VMEM((CH * Q, CH * B), jnp.bfloat16),
            pltpu.VMEM((DESC, CH, B, B), jnp.bfloat16),
            pltpu.VMEM((DESC, CH, Q, B), jnp.bfloat16),
            pltpu.VMEM((DESC, CH, Q, B), jnp.bfloat16),
            pltpu.VMEM((NX, 2 * DESC, HALF), jnp.float32),
            pltpu.VMEM((NY * NZ, 2, 2 * DESC, HALF), jnp.float32),
            pltpu.VMEM((HALF, B), jnp.bfloat16),
            pltpu.SMEM((NY * NZ * 2,), jnp.int32),
            pltpu.SMEM((DESC, CH), jnp.int32),
            pltpu.VMEM((DESC, Q), jnp.float32),
            pltpu.VMEM((1, B), jnp.int32),
            pltpu.SemaphoreType.DMA((SEMS,)),
            pltpu.SemaphoreType.DMA((SEMS,)),
            pltpu.SemaphoreType.DMA((2 * DESC + 2,)),
            pltpu.SemaphoreType.DMA((4,)),
        ],
        compiler_params=pltpu.CompilerParams(
            collective_id=0, has_side_effects=True, vmem_limit_bytes=56 * 1024 * 1024
        ),
    )(subtree_of, panel_mask, inv_diagonal, partition_order.reshape(1, B), sigma_tiles, panel_factor)
    return -product, variance.reshape(B)


def solution(mesh):
    placed = (
        P("leaf", "panel", None),
        P("leaf", None, "panel", None),
        P("leaf", None),
        P("leaf", "panel"),
        P(),
        P(("leaf", "panel")),
    )
    return jax.shard_map(
        body,
        mesh=mesh,
        in_specs=placed,
        out_specs=(P("leaf", None, "panel", None), P(("leaf", "panel"))),
        check_vma=False,
    )
```
